256 devices in a mesh: rows: 64 (over z, y_hi, x), cols: 4 (over y_lo, core).
Axes of the slice: x: 4, y: 4 (y_hi: 2, y_lo: 2; y = y_hi * 2 + y_lo), z: 8, core: 2. Of those that a mesh axis runs over, the one named last changes fastest.
Arguments:
- images: bfloat16 [2, 96, 256, 512], P(None, None, 'rows', 'cols'), may hold values from -6 to 6
- conv_weight: bfloat16 [128, 864], replicated, may hold values from -0.048112522 to 0.048112522
- conv_bias: float32 [128], replicated, may hold values from -0.15 to 0.15
- proj_weight: bfloat16 [256, 128], replicated, may hold values from -0.125 to 0.125
- proj_bias: float32 [256], replicated, may hold values from -1.2 to 1.2
Outputs:
- level_zero: bfloat16 [32768, 32768], P('rows', 'cols')
- level_one: bfloat16 [32768, 8192], P('rows', 'cols')
- level_two: bfloat16 [32768, 2048], P('rows', 'cols')
- level_three: bfloat16 [32768, 512], P('rows', 'cols')
The draws below stay inside these ranges and needn't reach their ends.
All inputs are finite; a program needn't handle non-finite values.
Results may differ from the reference program's by a relative error of at most 0.0039.
Values may be sent and summed in bfloat16 or wider, within the bound.
No kernel may reach another device: no remote copies, remote signals or barrier semaphores. Data moves between devices by JAX's collectives and lax.ppermute only.
A program may use at most 128 MiB of HBM per device.

```python
import math
import jax
import jax.numpy as jnp
from jax import lax

CIN = 96
CMID = 128
COUT = 256
BLOCK_W = 64
H8 = 128
W8 = 256
PIX = 32768
N_COLS = 4


def cosine_rows(key, row_count, row_length, squared_norm):
    choose_key, row_key, column_key = jax.random.split(key, 3)
    frequency = jax.random.permutation(choose_key, row_length - 1)[:row_count] + 1
    row_signs = (jax.random.randint(row_key, (row_count,), 0, 2) * 2 - 1).astype(jnp.float32)
    column_signs = (jax.random.randint(column_key, (row_length,), 0, 2) * 2 - 1).astype(jnp.float32)
    positions = 2 * jnp.arange(row_length, dtype=jnp.int32) + 1
    phases = frequency[:, None].astype(jnp.int32) * positions[None, :] % (4 * row_length)
    angles = phases.astype(jnp.float32) * (math.pi / (2.0 * row_length))
    cosine_table = jnp.cos(angles) * math.sqrt(2.0 * squared_norm / row_length)
    return cosine_table * row_signs[:, None] * column_signs[None, :]


def draw_conv_weight(key, part):
    key = jax.random.fold_in(key, 11)
    return cosine_rows(key, CMID, 9 * CIN, 1.0).astype(jnp.bfloat16)


def draw_proj_weight(key, part):
    key = jax.random.fold_in(key, 23)
    return cosine_rows(key, CMID, COUT, 2.0).T.astype(jnp.bfloat16)


def level_of(key, extent, cuts, low, high):
    gain = 1.0
    for position, shards_of in cuts:
        draws = jax.random.uniform(jax.random.fold_in(jax.random.fold_in(key, 6), position), (shards_of,), jnp.float32, low / len(cuts), high / len(cuts))
        gain = gain * jnp.repeat(jnp.exp(draws), extent[position] // shards_of).reshape((-1,) + (1,) * (len(extent) - 1 - position))
    return gain


def gaussian(key, shape, scale, bound, cuts=(), kind=jnp.bfloat16):
    drawn = scale * jax.random.normal(key, shape, jnp.float32)
    if cuts:
        drawn = drawn * level_of(key, shape, cuts, -0.22, 0.18)
    return jnp.clip(drawn, -bound, bound).astype(kind)


def setup_inputs(seed: int = 0) -> dict:
    seeds = jax.random.split(jax.random.key(seed), 6)
    images = gaussian(seeds[0], (2, CIN, 2 * H8, 2 * W8), 1.0, 6.0, ((2, 64), (3, 4)))
    conv_weight = draw_conv_weight(jax.random.fold_in(seeds[5], 71), 0)
    conv_bias = jnp.clip(jax.random.uniform(seeds[2], (CMID,), jnp.float32, -0.15, 0.15), -0.15, 0.15)
    proj_weight = draw_proj_weight(jax.random.fold_in(seeds[5], 71), 0)
    proj_bias = gaussian(seeds[4], (COUT,), 0.2, 1.2, (), jnp.float32)
    return dict(images=images, conv_weight=conv_weight, conv_bias=conv_bias, proj_weight=proj_weight, proj_bias=proj_bias)


def tap_columns(extended, out_rows, out_cols):
    slices = []
    for row_off in range(3):
        for col_off in range(3):
            slices.append(extended[..., row_off:row_off + 2 * out_rows - 1:2, col_off:col_off + 2 * out_cols - 1:2])
    stacked = jnp.stack(slices, axis=-4)
    lead = stacked.shape[:-4]
    return stacked.reshape(lead + (9 * extended.shape[-3], out_rows * out_cols))


def pool_level(volume, blocks, rows_h, cols_w):
    pixels = volume.shape[0]
    grouped = volume.astype(jnp.float32).reshape(pixels, blocks, rows_h // 2, 2, cols_w // 2, 2)
    pooled = jnp.sum(grouped, axis=(3, 5)) * 0.25
    return pooled.astype(jnp.bfloat16).reshape(pixels, -1)


def reference(images, conv_weight, conv_bias, proj_weight, proj_bias):
    padded = jnp.pad(images, ((0, 0), (0, 0), (1, 0), (1, 0)))
    tap_stack = tap_columns(padded, H8, W8).astype(jnp.float32)
    pre = jnp.einsum("ok,fkp->fop", conv_weight.astype(jnp.float32), tap_stack, precision=lax.Precision.HIGHEST)
    hidden = jnp.maximum(pre + conv_bias[None, :, None], 0.0).astype(jnp.bfloat16)
    feats = jnp.einsum("oc,fcp->fop", proj_weight.astype(jnp.float32), hidden.astype(jnp.float32), precision=lax.Precision.HIGHEST)
    feats = (feats + proj_bias[None, :, None]).astype(jnp.bfloat16)
    first_feats = feats[0].astype(jnp.float32)
    second_feats = feats[1].reshape(COUT, H8, N_COLS, BLOCK_W).transpose(0, 2, 1, 3).reshape(COUT, PIX).astype(jnp.float32)
    score_scale = COUT ** -0.5
    band_rows = first_feats.reshape(COUT, H8, W8).transpose(1, 0, 2)

    def one_band(band):
        level_zero = (jnp.dot(band.T, second_feats, precision=lax.Precision.HIGHEST) * score_scale).astype(jnp.bfloat16)
        level_one = pool_level(level_zero, N_COLS, H8, BLOCK_W)
        level_two = pool_level(level_one, N_COLS, H8 // 2, BLOCK_W // 2)
        level_three = pool_level(level_two, N_COLS, H8 // 4, BLOCK_W // 4)
        return level_zero, level_one, level_two, level_three

    outs = lax.map(one_band, band_rows)
    return (outs[0].reshape(PIX, -1), outs[1].reshape(PIX, -1), outs[2].reshape(PIX, -1), outs[3].reshape(PIX, -1))
```

```python
import jax
import jax.numpy as jnp
from jax import lax
from jax.experimental import pallas as pl
from jax.experimental.pallas import tpu as pltpu
from jax.sharding import PartitionSpec as P

PLANE = 8


def shifted(value, axis, steps):
    count = lax.axis_size(axis)
    first, last = (max(0, -steps), min(count, count - steps))
    return lax.ppermute(value, axis, [(source, source + steps) for source in range(first, last)])


def tap_columns(extended, out_rows, out_cols):
    slices = []
    for row_off in range(3):
        for col_off in range(3):
            slices.append(
                extended[
                    ...,
                    row_off : row_off + 2 * out_rows - 1 : 2,
                    col_off : col_off + 2 * out_cols - 1 : 2,
                ]
            )
    stacked = jnp.stack(slices, axis=-4)
    lead = stacked.shape[:-4]
    return stacked.reshape(lead + (9 * extended.shape[-3], out_rows * out_cols))


def hidden_of(extended, conv_weight, conv_bias, out_rows, out_cols):
    tap_stack = tap_columns(extended, out_rows, out_cols)
    pre = jnp.einsum("ok,...kp->...op", conv_weight, tap_stack, preferred_element_type=jnp.float32)
    return jnp.maximum(pre + conv_bias[:, None], 0.0).astype(jnp.bfloat16)


def feats_one_kernel(hid_ref, weight_ref, bias_ref, out_ref):
    for k in range(4):
        feats = lax.dot_general(
            hid_ref[k], weight_ref[...], (((0,), (1,)), ((), ())), preferred_element_type=jnp.float32
        )
        feats = (feats + bias_ref[...]).astype(jnp.bfloat16) * jnp.bfloat16(0.0625)
        for i in range(2):
            out_ref[i * 256 + k * 64 : i * 256 + (k + 1) * 64, :] = feats[i * 64 : (i + 1) * 64, :]


def feats_one(hidden, proj_weight, proj_bias):
    return pl.pallas_call(
        feats_one_kernel,
        out_shape=jax.ShapeDtypeStruct((512, 256), jnp.bfloat16),
        name="feats_one",
    )(hidden, proj_weight, proj_bias[None, :])


def plane_kernel(place_ref, first_ref, u_ref, v_ref, weight_ref, bias_ref, pool1_ref, pool2_ref, pool3_ref, *rest):
    zero_ref, one_ref, small_ref, one_scr = rest[-4:]
    step = pl.program_id(0)
    hid = jnp.where(step == 0, u_ref[...], v_ref[...])
    hid = jnp.concatenate([hid[j] for j in range(4)], axis=1)
    feats = jnp.dot(weight_ref[...], hid, preferred_element_type=jnp.float32)
    feats = (feats + bias_ref[...]).astype(jnp.bfloat16)
    zero = jnp.dot(first_ref[...], feats, preferred_element_type=jnp.float32).astype(jnp.bfloat16)
    zero_ref[...] = zero
    one = jnp.dot(zero, pool1_ref[...], preferred_element_type=jnp.float32).astype(jnp.bfloat16)
    one_ref[...] = one
    one_scr[step] = one

    @pl.when(step == 1)
    def _():
        whole = jnp.concatenate([one_scr[0], one_scr[1]], axis=1)
        two = jnp.dot(whole, pool2_ref[...], preferred_element_type=jnp.float32).astype(jnp.bfloat16)
        three = jnp.dot(two, pool3_ref[...], preferred_element_type=jnp.float32).astype(jnp.bfloat16)
        small_ref[0] = jnp.concatenate([two, three], axis=1)


def plane_call(place, first, u, u_block, v, v_block, consts, outs):
    full = lambda *shape: pl.BlockSpec(shape, lambda s, place: (0,) * len(shape))
    in_specs = [
        full(512, 256),
        pl.BlockSpec((4, 128, 128), lambda s, place: (u_block, 0, 0)),
        pl.BlockSpec((4, 128, 128), lambda s, place: (v_block, 0, 0)),
        full(256, 128),
        full(256, 1),
        full(512, 128),
        full(256, 64),
        full(64, 64),
    ]
    args = [place, first, u, v, *consts]
    aliases = {}
    if outs is not None:
        in_specs += [pl.BlockSpec(memory_space=pl.ANY)] * 3
        aliases = {len(args) + n: n for n in range(3)}
        args += list(outs)
    return pl.pallas_call(
        plane_kernel,
        grid_spec=pltpu.PrefetchScalarGridSpec(
            num_scalar_prefetch=1,
            grid=(2,),
            in_specs=in_specs,
            out_specs=[
                pl.BlockSpec((512, 512), lambda s, place: (0, 2 * place[0] + s)),
                pl.BlockSpec((512, 128), lambda s, place: (0, 2 * place[0] + s)),
                pl.BlockSpec((1, 512, 128), lambda s, place: (place[0], 0, 0)),
            ],
            scratch_shapes=[pltpu.VMEM((2, 512, 128), jnp.bfloat16)],
        ),
        out_shape=[
            jax.ShapeDtypeStruct((512, 8192), jnp.bfloat16),
            jax.ShapeDtypeStruct((512, 2048), jnp.bfloat16),
            jax.ShapeDtypeStruct((8, 512, 128), jnp.bfloat16),
        ],
        input_output_aliases=aliases,
        cost_estimate=pl.CostEstimate(flops=1_400_000_000, bytes_accessed=4_000_000, transcendentals=0),
        name="plane",
    )(*args)


def last_kernel(small_ref, two_ref, three_ref):
    for z in range(8):
        two_ref[:, z * 64 : (z + 1) * 64] = small_ref[z, :, 0:64]
        three_ref[:, z * 16 : (z + 1) * 16] = small_ref[z, :, 64:80]


def pool_matrix(rows, cols, pad):
    pixel = lax.broadcasted_iota(jnp.int32, (rows * cols, pad), 0)
    cell = lax.broadcasted_iota(jnp.int32, (rows * cols, pad), 1)
    own = (pixel // cols // 2) * (cols // 2) + (pixel % cols) // 2
    return jnp.where(own == cell, 0.25, 0.0).astype(jnp.bfloat16)


def per_device(images, conv_weight, conv_bias, proj_weight, proj_bias):
    in_rows = images.shape[2]
    in_cols = images.shape[3]
    out_rows = in_rows // 2
    out_cols = in_cols // 2
    n_rows = lax.axis_size("rows")
    left_rim = shifted(images[:, :, :, in_cols - 1 :], "cols", 1)
    widened = jnp.concatenate([left_rim, images], axis=3)
    top_rim = shifted(widened[:, :, in_rows - 1 :, :], "rows", 1)
    extended = jnp.concatenate([top_rim, widened], axis=2)
    hidden = hidden_of(extended, conv_weight, conv_bias, out_rows, out_cols)

    plane_groups = [[z * PLANE + n for n in range(PLANE)] for z in range(n_rows // PLANE)]
    mine = lax.all_to_all(
        jnp.broadcast_to(hidden[1][None], (PLANE,) + hidden[1].shape),
        "rows", 0, 0, axis_index_groups=plane_groups,
    )
    band = lax.all_to_all(jnp.broadcast_to(hidden[0][None], (4,) + hidden[0].shape), "cols", 0, 0)

    up = [(r, (r + PLANE) % n_rows) for r in range(n_rows)]
    down = [(r, (r - PLANE) % n_rows) for r in range(n_rows)]
    z = lax.axis_index("rows") // PLANE
    planes = n_rows // PLANE
    place = lambda off: jnp.reshape((z + off) % planes, (1,)).astype(jnp.int32)

    first = feats_one(band, proj_weight, proj_bias)
    consts = (
        proj_weight,
        proj_bias[:, None],
        pool_matrix(8, 64, 128),
        pool_matrix(8, 32, 64),
        pool_matrix(4, 16, 64),
    )
    below, above = mine, mine
    outs = plane_call(place(0), first, mine, 0, mine, 1, consts, None)
    for off in range(1, planes // 2):
        below = lax.ppermute(below, "rows", up)
        above = lax.ppermute(above, "rows", down)
        outs = plane_call(place(-off), first, below, 0, below, 1, consts, outs)
        outs = plane_call(place(off), first, above, 0, above, 1, consts, outs)
    below = lax.ppermute(below[:4], "rows", up)
    above = lax.ppermute(above[4:], "rows", down)
    outs = plane_call(place(planes // 2), first, below, 0, above, 0, consts, outs)
    level_two, level_three = pl.pallas_call(
        last_kernel,
        out_shape=[
            jax.ShapeDtypeStruct((512, 512), jnp.bfloat16),
            jax.ShapeDtypeStruct((512, 128), jnp.bfloat16),
        ],
        name="small_levels",
    )(outs[2])
    return (outs[0], outs[1], level_two, level_three)


def solution(mesh):
    in_specs = (P(None, None, "rows", "cols"), P(), P(), P(), P())
    out_specs = (P("rows", "cols"), P("rows", "cols"), P("rows", "cols"), P("rows", "cols"))
    return jax.shard_map(
        per_device, mesh=mesh, in_specs=in_specs, out_specs=out_specs, check_vma=False
    )
```

```python
import functools

import jax
import jax.numpy as jnp
from jax import lax
from jax.experimental import pallas as pl
from jax.experimental.pallas import tpu as pltpu
from jax.sharding import PartitionSpec as P

Z, YH, X = 8, 2, 4
PLANE = YH * X
ROWS, COLS = Z * PLANE, 4
BF, F32 = jnp.bfloat16, jnp.float32


def dot(a, b):
    return jnp.dot(a, b, preferred_element_type=F32)


def iotas(*shape):
    return lax.broadcasted_iota(jnp.int32, shape, 0), lax.broadcasted_iota(jnp.int32, shape, 1)


def one_hot(mask, value=1.0):
    return jnp.where(mask, value, 0.0).astype(BF)


def split_kernel(tile_ref, main_ref, top_ref, left_ref, corner_ref):
    row, col = iotas(384, 384)
    tap = (row >= 96).astype(jnp.int32) + (row >= 192).astype(jnp.int32) + (row >= 288).astype(jnp.int32)
    order = one_hot(col == (row - 96 * tap) * 4 + tap)
    main = dot(order, jnp.concatenate([tile_ref[0], tile_ref[1]], axis=1)).astype(BF)
    row, col = iotas(256, 128)
    rim = one_hot(((row == 127) & (col == 0)) | ((row == 255) & (col == 64)))
    left = dot(main, rim).astype(BF)
    main_ref[...] = main
    top_ref[...] = main[288:384]
    left_ref[...] = left
    corner_ref[...] = left[288:384]


def split_tile(images):
    return pl.pallas_call(
        split_kernel,
        out_shape=[
            jax.ShapeDtypeStruct((384, 256), BF),
            jax.ShapeDtypeStruct((96, 256), BF),
            jax.ShapeDtypeStruct((384, 128), BF),
            jax.ShapeDtypeStruct((96, 128), BF),
        ],
        name="split_tile",
    )(images.reshape(2, 384, 128))


def hidden_kernel(main_ref, top_ref, left_ref, corner_ref, weight_ref, bias_ref, one_ref, two_ref):
    rows = jnp.concatenate([top_ref[...], main_ref[...]], axis=0)
    row, col = iotas(256, 384)
    source = 2 * (col & 63) - 1 + (col >> 7) + jnp.where((col & 64) != 0, 128, 0)
    valid = ((col & 63) != 0) | (col >= 128)
    taps = dot(rows, one_hot((row == source) & valid))
    rim = jnp.concatenate([corner_ref[...], left_ref[...]], axis=0).astype(F32)
    first = (taps[:, :128] + rim).astype(BF)
    parts = [first, taps[:, 128:256].astype(BF), taps[:, 256:384].astype(BF)]
    stacked = jnp.concatenate(
        [
            jnp.concatenate(
                [parts[b][(2 * i + a) * 96 : (2 * i + a + 1) * 96] for a in range(3) for b in range(3)], axis=0
            )
            for i in range(2)
        ],
        axis=1,
    )
    pre = dot(weight_ref[...], stacked)
    bias = jnp.transpose(jnp.broadcast_to(bias_ref[...], (128, 128)))
    hidden = [jnp.maximum(pre[:, i * 128 : (i + 1) * 128] + bias, 0.0) for i in range(2)]
    lane = lax.broadcasted_iota(jnp.int32, (128, 128), 1)
    one_ref[...] = jnp.where(lane < 64, hidden[0], pltpu.roll(hidden[1], 64, 1)).astype(BF)
    two_ref[...] = jnp.where(lane < 64, pltpu.roll(hidden[0], 64, 1), hidden[1]).astype(BF)


def hidden_of(main, top, left, corner, conv_weight, conv_bias):
    return pl.pallas_call(
        hidden_kernel,
        out_shape=[jax.ShapeDtypeStruct((128, 128), BF)] * 2,
        name="hidden",
    )(main, top, left, corner, conv_weight, conv_bias[None, :])


def feats_one_kernel(meta_ref, *refs):
    hid_refs, (weight_ref, bias_ref, out_ref) = refs[:4], refs[4:]
    for m in range(4):
        k = meta_ref[9] ^ m
        feats = lax.dot_general(
            hid_refs[m][...], weight_ref[...], (((0,), (1,)), ((), ())), preferred_element_type=F32
        )
        feats = (feats + bias_ref[...]).astype(BF) * jnp.bfloat16(0.0625)
        for i in range(2):
            out_ref[pl.ds(pl.multiple_of(i * 256 + k * 64, 64), 64), :] = feats[i * 64 : (i + 1) * 64, :]


def feats_one(meta, hidden, proj_weight, proj_bias):
    vmem, smem = pl.BlockSpec(memory_space=pltpu.VMEM), pl.BlockSpec(memory_space=pltpu.SMEM)
    return pl.pallas_call(
        feats_one_kernel,
        in_specs=[smem] + [vmem] * 6,
        out_shape=jax.ShapeDtypeStruct((512, 256), BF),
        name="feats_one",
    )(meta, *hidden, proj_weight, proj_bias[None, :])


def planes_kernel(offsets, halves, n_alias, meta_ref, first_ref, weight_ref, bias_ref, *refs):
    hid_refs, rest = refs[: len(offsets) * halves], refs[len(offsets) * halves + n_alias :]
    zero_out, one_out, small_out, zero_buf, one_buf, small_buf, hid_buf, sems = rest
    row, col = iotas(512, 128)
    pool1 = one_hot(col == (row >> 7) * 32 + ((row & 63) >> 1), 0.25)
    row, col = iotas(256, 64)
    pool2 = one_hot(col == (row >> 6) * 16 + ((row & 31) >> 1), 0.25)
    row, col = iotas(64, 64)
    pool3 = one_hot(col == (row >> 5) * 8 + ((row & 15) >> 1), 0.25)
    bias = jnp.concatenate(
        [jnp.transpose(jnp.broadcast_to(bias_ref[n : n + 1, :], (128, 128))) for n in range(2)], axis=0
    )
    bias = jnp.concatenate([bias] * 4, axis=1)
    copies = []

    def send(source, target):
        copies.append(pltpu.make_async_copy(source, target, sems.at[len(copies)]))
        copies[-1].start()

    for n, offset in enumerate(offsets):
        place = (meta_ref[0] + (offset + Z)) & (Z - 1)
        if halves == 2:
            hid_buf[0:4] = hid_refs[0][...]
            hid_buf[4:8] = hid_refs[1][...]
            hid_ref = hid_buf
        else:
            hid_ref = hid_refs[n]
        ones = []
        for half in range(2):
            hid = jnp.concatenate([hid_ref[meta_ref[1 + 4 * half + j]] for j in range(4)], axis=1)
            feats = (dot(weight_ref[...], hid) + bias).astype(BF)
            zero = dot(first_ref[...], feats).astype(BF)
            slot = 2 * n + half
            zero_buf[slot] = zero
            send(zero_buf.at[slot], zero_out.at[:, pl.ds(pl.multiple_of(place * 1024 + half * 512, 512), 512)])
            ones.append(dot(zero, pool1).astype(BF))
        one = jnp.concatenate(ones, axis=1)
        one_buf[n] = one
        send(one_buf.at[n], one_out.at[:, pl.ds(pl.multiple_of(place * 256, 256), 256)])
        two = dot(one, pool2).astype(BF)
        three = dot(two, pool3).astype(BF)
        small_buf[n] = jnp.concatenate([two, three], axis=1)
        send(small_buf.at[n], small_out.at[place])
    for copy in copies:
        copy.wait()


def planes_call(offsets, hidden, meta, first, proj_weight, proj_bias, outs):
    halves = len(hidden) // len(offsets)
    count = len(offsets)
    args = [meta, first, proj_weight, proj_bias.reshape(2, 128), *hidden]
    vmem, smem = pl.BlockSpec(memory_space=pltpu.VMEM), pl.BlockSpec(memory_space=pltpu.SMEM)
    anywhere = pl.BlockSpec(memory_space=pl.ANY)
    in_specs = [smem] + [vmem] * (len(args) - 1)
    aliases = {}
    if outs is not None:
        aliases = {len(args) + n: n for n in range(3)}
        args += list(outs)
        in_specs += [anywhere] * 3
    return pl.pallas_call(
        functools.partial(planes_kernel, offsets, halves, len(aliases)),
        in_specs=in_specs,
        out_specs=[anywhere] * 3,
        out_shape=[
            jax.ShapeDtypeStruct((512, 8192), BF),
            jax.ShapeDtypeStruct((512, 2048), BF),
            jax.ShapeDtypeStruct((8, 512, 128), BF),
        ],
        scratch_shapes=[
            pltpu.VMEM((2 * count, 512, 512), BF),
            pltpu.VMEM((count, 512, 256), BF),
            pltpu.VMEM((count, 512, 128), BF),
            pltpu.VMEM((8, 128, 128), BF),
            pltpu.SemaphoreType.DMA((4 * count,)),
        ],
        input_output_aliases=aliases,
        compiler_params=pltpu.CompilerParams(vmem_limit_bytes=24 << 20),
        cost_estimate=pl.CostEstimate(
            flops=1_400_000_000 * count, bytes_accessed=1_500_000 * count, transcendentals=0
        ),
        name="planes",
    )(*args)


def last_kernel(small_ref, two_ref, three_ref):
    for z in range(Z):
        two_ref[:, z * 64 : (z + 1) * 64] = small_ref[z, :, 0:64]
        three_ref[:, z * 16 : (z + 1) * 16] = small_ref[z, :, 64:80]


def per_device(images, conv_weight, conv_bias, proj_weight, proj_bias):
    right = [(c, c + 1) for c in range(COLS - 1)]
    down = [(r, r + 1) for r in range(ROWS - 1)]
    diagonal = [(r * COLS + c, (r + 1) * COLS + c + 1) for r in range(ROWS - 1) for c in range(COLS - 1)]
    main, top, left, corner = split_tile(images)
    top = lax.ppermute(top, "rows", down)
    left = lax.ppermute(left, "cols", right)
    corner = lax.ppermute(corner, ("rows", "cols"), diagonal)
    hidden_one, hidden_two = hidden_of(main, top, left, corner, conv_weight, conv_bias)

    r, c = lax.axis_index("rows"), lax.axis_index("cols")
    z, yh, x = r // PLANE, (r // X) % YH, r % X
    order = [((j % X - x) % X) * 2 + (yh ^ (j // X)) for j in range(PLANE)]
    meta = jnp.stack([z, *order, c] + [jnp.int32(0)] * 6).astype(jnp.int32)

    def along(axis, steps):
        size, stride = {"z": (Z, PLANE), "yh": (YH, X), "x": (X, 1)}[axis]
        target = lambda r: r + ((r // stride + steps) % size - (r // stride) % size) * stride
        return [(r, target(r)) for r in range(ROWS)]

    other = lax.ppermute(hidden_two, "rows", along("yh", 1))
    pair = jnp.stack([hidden_two, other])
    ones = [hidden_one]
    ones += [lax.ppermute(hidden_one, "cols", [(k, k ^ m) for k in range(COLS)]) for m in range(1, 4)]
    mine = jnp.concatenate([pair] + [lax.ppermute(pair, "rows", along("x", -s)) for s in range(1, X)])
    first = feats_one(meta, ones, proj_weight, proj_bias)

    call = functools.partial(planes_call, meta=meta, first=first, proj_weight=proj_weight, proj_bias=proj_bias)
    below, above = mine, mine
    outs = call((0,), [mine], outs=None)
    for step in range(1, Z // 2):
        below = lax.ppermute(below, "rows", along("z", 1))
        above = lax.ppermute(above, "rows", along("z", -1))
        outs = call((-step, step), [below, above], outs=outs)
    below = lax.ppermute(below[:4], "rows", along("z", 1))
    above = lax.ppermute(above[4:], "rows", along("z", -1))
    outs = call((Z // 2,), [below, above], outs=outs)
    level_two, level_three = pl.pallas_call(
        last_kernel,
        out_shape=[jax.ShapeDtypeStruct((512, 512), BF), jax.ShapeDtypeStruct((512, 128), BF)],
        name="small_levels",
    )(outs[2])
    return (outs[0], outs[1], level_two, level_three)


def solution(mesh):
    in_specs = (P(None, None, "rows", "cols"), P(), P(), P(), P())
    out_specs = (P("rows", "cols"), P("rows", "cols"), P("rows", "cols"), P("rows", "cols"))
    return jax.shard_map(
        per_device, mesh=mesh, in_specs=in_specs, out_specs=out_specs, check_vma=False
    )
```

```python
import functools

import jax
import jax.numpy as jnp
from jax import lax
from jax.experimental import pallas as pl
from jax.experimental.pallas import tpu as pltpu
from jax.sharding import PartitionSpec as P

Z, YH, X = 8, 2, 4
PLANE = YH * X
ROWS, COLS = Z * PLANE, 4
BF, F32 = jnp.bfloat16, jnp.float32


def dot(a, b):
    return jnp.dot(a, b, preferred_element_type=F32)


def iotas(*shape):
    return lax.broadcasted_iota(jnp.int32, shape, 0), lax.broadcasted_iota(jnp.int32, shape, 1)


def position():
    r = lax.axis_index("rows")
    return r // PLANE, r // X % YH, r % X


VMEM, SMEM = pl.BlockSpec(memory_space=pltpu.VMEM), pl.BlockSpec(memory_space=pltpu.SMEM)
ANYWHERE = pl.BlockSpec(memory_space=pl.ANY)
SMALL = pltpu.CompilerParams(vmem_limit_bytes=12 << 20)


def one_hot(mask, value=1.0):
    return jnp.where(mask, value, 0.0).astype(BF)


def split_kernel(tile_ref, main_ref, left_ref):
    row, col = iotas(384, 384)
    tap = (row >= 96).astype(jnp.int32) + (row >= 192).astype(jnp.int32) + (row >= 288).astype(jnp.int32)
    order = one_hot(col == (row - 96 * tap) * 4 + tap)
    main = dot(order, jnp.concatenate([tile_ref[0], tile_ref[1]], axis=1)).astype(BF)
    row, col = iotas(256, 128)
    rim = one_hot(((row == 127) & (col == 0)) | ((row == 255) & (col == 64)))
    main_ref[...] = main
    left_ref[...] = dot(main, rim).astype(BF)


def split_tile(images):
    return pl.pallas_call(
        split_kernel,
        out_shape=[jax.ShapeDtypeStruct((384, 256), BF), jax.ShapeDtypeStruct((384, 128), BF)],
        compiler_params=SMALL,
        name="split_tile",
    )(images.reshape(2, 384, 128))


def hidden_kernel(main_ref, top_ref, left_ref, weight_ref, bias_ref, one_ref, two_ref):
    rows = jnp.concatenate([top_ref[:, :256], main_ref[...]], axis=0)
    row, col = iotas(256, 384)
    source = 2 * (col & 63) - 1 + (col >> 7) + jnp.where((col & 64) != 0, 128, 0)
    valid = ((col & 63) != 0) | (col >= 128)
    taps = dot(rows, one_hot((row == source) & valid))
    rim = jnp.concatenate([top_ref[:, 256:], left_ref[...]], axis=0).astype(F32)
    first = (taps[:, :128] + rim).astype(BF)
    parts = [first, taps[:, 128:256].astype(BF), taps[:, 256:384].astype(BF)]
    stacked = jnp.concatenate(
        [
            jnp.concatenate(
                [parts[b][(2 * i + a) * 96 : (2 * i + a + 1) * 96] for a in range(3) for b in range(3)], axis=0
            )
            for i in range(2)
        ],
        axis=1,
    )
    pre = lax.dot_general(weight_ref[...], stacked, (((0,), (0,)), ((), ())), preferred_element_type=F32)
    bias = jnp.transpose(jnp.broadcast_to(bias_ref[...], (128, 128)))
    hidden = [jnp.maximum(pre[:, i * 128 : (i + 1) * 128] + bias, 0.0) for i in range(2)]
    lane = lax.broadcasted_iota(jnp.int32, (128, 128), 1)
    one_ref[...] = jnp.where(lane < 64, hidden[0], pltpu.roll(hidden[1], 64, 1)).astype(BF)
    two_ref[...] = jnp.where(lane < 64, pltpu.roll(hidden[0], 64, 1), hidden[1]).astype(BF)


def hidden_of(main, top, left, conv_weight, conv_bias):
    return pl.pallas_call(
        hidden_kernel,
        out_shape=[jax.ShapeDtypeStruct((128, 128), BF)] * 2,
        compiler_params=SMALL,
        name="hidden",
    )(main, top, left, conv_weight.T, conv_bias[None, :])


def feats_one_kernel(*refs):
    hid_refs, (weight_ref, bias_ref, out_ref) = refs[:4], refs[4:]
    for m in range(4):
        k = lax.axis_index("cols") ^ m
        feats = lax.dot_general(
            hid_refs[m][...], weight_ref[...], (((0,), (1,)), ((), ())), preferred_element_type=F32
        )
        feats = (feats + bias_ref[...]).astype(BF) * jnp.bfloat16(0.0625)
        for i in range(2):
            out_ref[pl.ds(pl.multiple_of(i * 256 + k * 64, 64), 64), :] = feats[i * 64 : (i + 1) * 64, :]


def feats_one(hidden, proj_weight, proj_bias):
    return pl.pallas_call(
        feats_one_kernel,
        out_shape=jax.ShapeDtypeStruct((512, 256), BF),
        compiler_params=SMALL,
        name="feats_one",
    )(*hidden, proj_weight, proj_bias[None, :])


def planes_kernel(offsets, last, n_alias, first_ref, weight_ref, bias_ref, *refs):
    n_hid = 2 if last else len(offsets)
    hid_refs, rest = refs[:n_hid], refs[n_hid + n_alias :]
    if last:
        small_ref, zero_out, one_out, two_out, three_out, zero_buf, one_buf, two_buf, three_buf, hid_buf, sems = rest
    else:
        zero_out, one_out, small_out, zero_buf, one_buf, small_buf, sems = rest
    z, yh, x = position()
    order = [((j % X - x) & (X - 1)) * 2 + (yh ^ (j // X)) for j in range(PLANE)]
    row, col = iotas(512, 128)
    pool1 = one_hot(col == (row >> 7) * 32 + ((row & 63) >> 1), 0.25)
    row, col = iotas(256, 64)
    pool2 = one_hot(col == (row >> 6) * 16 + ((row & 31) >> 1), 0.25)
    row, col = iotas(64, 64)
    pool3 = one_hot(col == (row >> 5) * 8 + ((row & 15) >> 1), 0.25)
    bias = jnp.concatenate(
        [jnp.transpose(jnp.broadcast_to(bias_ref[n : n + 1, :], (128, 128))) for n in range(2)], axis=0
    )
    bias = jnp.concatenate([bias] * 4, axis=1)
    copies = []

    def send(source, target):
        copies.append(pltpu.make_async_copy(source, target, sems.at[len(copies)]))
        copies[-1].start()

    for n, offset in enumerate(offsets):
        place = (z + (offset + Z)) & (Z - 1)
        if last:
            hid_buf[0:4] = hid_refs[0][...]
            hid_buf[4:8] = hid_refs[1][...]
            hid_ref = hid_buf
        else:
            hid_ref = hid_refs[n]
        ones = []
        for half in range(2):
            hid = jnp.concatenate([hid_ref[order[4 * half + j]] for j in range(4)], axis=1)
            feats = (dot(weight_ref[...], hid) + bias).astype(BF)
            zero = dot(first_ref[...], feats).astype(BF)
            slot = 2 * n + half
            zero_buf[slot] = zero
            send(zero_buf.at[slot], zero_out.at[:, pl.ds(pl.multiple_of(place * 1024 + half * 512, 512), 512)])
            ones.append(dot(zero, pool1).astype(BF))
        one = jnp.concatenate(ones, axis=1)
        one_buf[n] = one
        send(one_buf.at[n], one_out.at[:, pl.ds(pl.multiple_of(place * 256, 256), 256)])
        two = dot(one, pool2).astype(BF)
        three = dot(two, pool3).astype(BF)
        small = jnp.concatenate([two, three], axis=1)
        if not last:
            small_buf[n] = small
            send(small_buf.at[n], small_out.at[place])
    if last:
        for m in range(Z):
            piece = jnp.where(place == m, small, small_ref[m])
            two_buf[:, m * 64 : (m + 1) * 64] = piece[:, 0:64]
            three_buf[:, m * 16 : (m + 1) * 16] = piece[:, 64:80]
        send(two_buf, two_out)
        send(three_buf, three_out)
    for copy in copies:
        copy.wait()


def planes_call(offsets, hidden, first, proj_weight, proj_bias, outs, last=False):
    count = len(offsets)
    args = [first, proj_weight, proj_bias.reshape(2, 128), *hidden]
    in_specs = [VMEM] * len(args)
    aliases = {}
    if outs is not None:
        shared = 2 if last else 3
        aliases = {len(args) + n: n for n in range(shared)}
        args += list(outs)
        in_specs += [ANYWHERE] * shared + [VMEM] * (3 - shared)
    shapes = [(512, 8192), (512, 2048)] + ([(512, 512), (512, 128)] if last else [(8, 512, 128)])
    scratch = [(2 * count, 512, 512), (count, 512, 256)]
    scratch += [(512, 512), (512, 128), (8, 128, 128)] if last else [(count, 512, 128)]
    return pl.pallas_call(
        functools.partial(planes_kernel, offsets, last, len(aliases)),
        in_specs=in_specs,
        out_specs=[ANYWHERE] * len(shapes),
        out_shape=[jax.ShapeDtypeStruct(shape, BF) for shape in shapes],
        scratch_shapes=[pltpu.VMEM(shape, BF) for shape in scratch] + [pltpu.SemaphoreType.DMA((5 * count,))],
        input_output_aliases=aliases,
        compiler_params=pltpu.CompilerParams(vmem_limit_bytes=24 << 20),
        cost_estimate=pl.CostEstimate(
            flops=1_400_000_000 * count, bytes_accessed=1_500_000 * count, transcendentals=0
        ),
        name="planes",
    )(*args)


def per_device(images, conv_weight, conv_bias, proj_weight, proj_bias):
    right = [(c, c + 1) for c in range(COLS - 1)]
    down = [(r, r + 1) for r in range(ROWS - 1)]
    main, left = split_tile(images)
    left = lax.ppermute(left, "cols", right)
    top = lax.ppermute(jnp.concatenate([main[288:], left[288:]], axis=1), "rows", down)
    hidden_one, hidden_two = hidden_of(main, top, left, conv_weight, conv_bias)

    def along(axis, steps):
        size, stride = {"z": (Z, PLANE), "yh": (YH, X), "x": (X, 1)}[axis]
        target = lambda r: r + ((r // stride + steps) % size - (r // stride) % size) * stride
        return [(r, target(r)) for r in range(ROWS)]

    other = lax.ppermute(hidden_two, "rows", along("yh", 1))
    pair = jnp.stack([hidden_two, other])
    ones = [hidden_one]
    ones += [lax.ppermute(hidden_one, "cols", [(k, k ^ m) for k in range(COLS)]) for m in range(1, 4)]
    mine = jnp.concatenate([pair] + [lax.ppermute(pair, "rows", along("x", -s)) for s in range(1, X)])
    mine, ones = lax.optimization_barrier((mine, ones))
    first = feats_one(ones, proj_weight, proj_bias)

    call = functools.partial(planes_call, first=first, proj_weight=proj_weight, proj_bias=proj_bias)
    below, above = mine, mine
    outs = call((0,), [mine], outs=None)
    for step in range(1, Z // 2):
        below = lax.ppermute(below, "rows", along("z", 1))
        above = lax.ppermute(above, "rows", along("z", -1))
        outs = call((-step, step), [below, above], outs=outs)
    below = lax.ppermute(below[:4], "rows", along("z", 1))
    above = lax.ppermute(above[4:], "rows", along("z", -1))
    return tuple(call((Z // 2,), [below, above], outs=outs, last=True))


def solution(mesh):
    in_specs = (P(None, None, "rows", "cols"), P(), P(), P(), P())
    out_specs = (P("rows", "cols"), P("rows", "cols"), P("rows", "cols"), P("rows", "cols"))
    return jax.shard_map(
        per_device, mesh=mesh, in_specs=in_specs, out_specs=out_specs, check_vma=False
    )
```

```python
import functools

import jax
import jax.numpy as jnp
from jax import lax
from jax.experimental import pallas as pl
from jax.experimental.pallas import tpu as pltpu
from jax.sharding import PartitionSpec as P

Z, YH, X = 8, 2, 4
PLANE = YH * X
ROWS, COLS = Z * PLANE, 4
BF, F32 = jnp.bfloat16, jnp.float32


def dot(a, b):
    return jnp.dot(a, b, preferred_element_type=F32)


def iotas(*shape):
    return lax.broadcasted_iota(jnp.int32, shape, 0), lax.broadcasted_iota(jnp.int32, shape, 1)


def position():
    r = lax.axis_index("rows")
    return r // PLANE, r // X % YH, r % X


VMEM, SMEM = pl.BlockSpec(memory_space=pltpu.VMEM), pl.BlockSpec(memory_space=pltpu.SMEM)
ANYWHERE = pl.BlockSpec(memory_space=pl.ANY)
SMALL = pltpu.CompilerParams(vmem_limit_bytes=12 << 20)


def one_hot(mask, value=1.0):
    return jnp.where(mask, value, 0.0).astype(BF)


def stage_kernel(*refs):
    count = len(refs) // 2
    copies = [pltpu.make_async_copy(refs[n], refs[count + n], refs[-1].at[n]) for n in range(count)]
    for copy in copies:
        copy.start()
    for copy in copies:
        copy.wait()


def stage(*params):
    return pl.pallas_call(
        stage_kernel,
        in_specs=[ANYWHERE] * len(params),
        out_shape=[jax.ShapeDtypeStruct(param.shape, param.dtype) for param in params],
        scratch_shapes=[pltpu.SemaphoreType.DMA((len(params),))],
        compiler_params=SMALL,
        cost_estimate=pl.CostEstimate(flops=1_000_000_000, bytes_accessed=600_000, transcendentals=0),
        name="stage",
    )(*params)


def split_kernel(tile_ref, main_ref, top_ref, left_ref, corner_ref):
    row, col = iotas(384, 384)
    tap = (row >= 96).astype(jnp.int32) + (row >= 192).astype(jnp.int32) + (row >= 288).astype(jnp.int32)
    order = one_hot(col == (row - 96 * tap) * 4 + tap)
    main = dot(order, jnp.concatenate([tile_ref[0], tile_ref[1]], axis=1)).astype(BF)
    row, col = iotas(256, 128)
    rim = one_hot(((row == 127) & (col == 0)) | ((row == 255) & (col == 64)))
    left = dot(main, rim).astype(BF)
    main_ref[...] = main
    top_ref[...] = main[288:384]
    left_ref[...] = left
    corner_ref[...] = left[288:384]


def split_tile(images):
    return pl.pallas_call(
        split_kernel,
        out_shape=[jax.ShapeDtypeStruct(shape, BF) for shape in ((384, 256), (96, 256), (384, 128), (96, 128))],
        compiler_params=SMALL,
        name="split_tile",
    )(images.reshape(2, 384, 128))


def hidden_kernel(main_ref, top_ref, left_ref, corner_ref, weight_ref, bias_ref, one_ref, two_ref):
    rows = jnp.concatenate([top_ref[...], main_ref[...]], axis=0)
    row, col = iotas(256, 384)
    source = 2 * (col & 63) - 1 + (col >> 7) + jnp.where((col & 64) != 0, 128, 0)
    valid = ((col & 63) != 0) | (col >= 128)
    taps = dot(rows, one_hot((row == source) & valid))
    rim = jnp.concatenate([corner_ref[...], left_ref[...]], axis=0).astype(F32)
    first = (taps[:, :128] + rim).astype(BF)
    parts = [first, taps[:, 128:256].astype(BF), taps[:, 256:384].astype(BF)]
    stacked = jnp.concatenate(
        [
            jnp.concatenate(
                [parts[b][(2 * i + a) * 96 : (2 * i + a + 1) * 96] for a in range(3) for b in range(3)], axis=0
            )
            for i in range(2)
        ],
        axis=1,
    )
    pre = lax.dot_general(weight_ref[...], stacked, (((0,), (0,)), ((), ())), preferred_element_type=F32)
    bias = jnp.transpose(jnp.broadcast_to(bias_ref[...], (128, 128)))
    hidden = [jnp.maximum(pre[:, i * 128 : (i + 1) * 128] + bias, 0.0) for i in range(2)]
    lane = lax.broadcasted_iota(jnp.int32, (128, 128), 1)
    one_ref[...] = jnp.where(lane < 64, hidden[0], pltpu.roll(hidden[1], 64, 1)).astype(BF)
    two_ref[...] = jnp.where(lane < 64, pltpu.roll(hidden[0], 64, 1), hidden[1]).astype(BF)


def hidden_of(main, top, left, corner, conv_weight, conv_bias):
    return pl.pallas_call(
        hidden_kernel,
        out_shape=[jax.ShapeDtypeStruct((128, 128), BF)] * 2,
        compiler_params=SMALL,
        name="hidden",
    )(main, top, left, corner, conv_weight, conv_bias)


def feats_one_kernel(*refs):
    hid_refs, (weight_ref, bias_ref, out_ref) = refs[:4], refs[4:]
    for m in range(4):
        k = lax.axis_index("cols") ^ m
        feats = lax.dot_general(
            hid_refs[m][...], weight_ref[...], (((0,), (1,)), ((), ())), preferred_element_type=F32
        )
        bias = jnp.concatenate([bias_ref[0:1, :], bias_ref[1:2, :]], axis=1)
        feats = (feats + bias).astype(BF) * jnp.bfloat16(0.0625)
        for i in range(2):
            out_ref[pl.ds(pl.multiple_of(i * 256 + k * 64, 64), 64), :] = feats[i * 64 : (i + 1) * 64, :]


def feats_one(hidden, proj_weight, proj_bias):
    return pl.pallas_call(
        feats_one_kernel,
        out_shape=jax.ShapeDtypeStruct((512, 256), BF),
        compiler_params=SMALL,
        name="feats_one",
    )(*hidden, proj_weight, proj_bias)


def planes_kernel(offsets, merge, last, n_alias, first_ref, weight_ref, bias_ref, *refs):
    n_hid = 2 if last else len(offsets)
    hid_refs, rest = refs[:n_hid], refs[n_hid + n_alias :]
    if merge:
        small_ref, zero_out, one_out, two_buf, three_buf, zero_buf, one_buf, sems = rest
    elif last:
        two_ref, three_ref, zero_out, one_out, two_out, three_out = rest[:6]
        zero_buf, one_buf, two_buf, three_buf, hid_buf, sems = rest[6:]
    else:
        zero_out, one_out, small_out, zero_buf, one_buf, small_buf, sems = rest
    z, yh, x = position()
    order = [((j % X - x) & (X - 1)) * 2 + (yh ^ (j // X)) for j in range(PLANE)]
    row, col = iotas(512, 128)
    pool1 = one_hot(col == (row >> 7) * 32 + ((row & 63) >> 1), 0.25)
    row, col = iotas(256, 64)
    pool2 = one_hot(col == (row >> 6) * 16 + ((row & 31) >> 1), 0.25)
    row, col = iotas(64, 64)
    pool3 = one_hot(col == (row >> 5) * 8 + ((row & 15) >> 1), 0.25)
    bias = jnp.concatenate(
        [jnp.transpose(jnp.broadcast_to(bias_ref[n : n + 1, :], (128, 128))) for n in range(2)], axis=0
    )
    bias = jnp.concatenate([bias] * 4, axis=1)
    copies, places, smalls = [], [], []

    def send(source, target):
        copies.append(pltpu.make_async_copy(source, target, sems.at[len(copies)]))
        copies[-1].start()

    for n, offset in enumerate(offsets):
        place = (z + (offset + Z)) & (Z - 1)
        if last:
            hid_buf[0:4] = hid_refs[0][...]
            hid_buf[4:8] = hid_refs[1][...]
            hid_ref = hid_buf
        else:
            hid_ref = hid_refs[n]
        ones = []
        for half in range(2):
            hid = jnp.concatenate([hid_ref[order[4 * half + j]] for j in range(4)], axis=1)
            feats = (dot(weight_ref[...], hid) + bias).astype(BF)
            zero = dot(first_ref[...], feats).astype(BF)
            slot = 2 * n + half
            zero_buf[slot] = zero
            send(zero_buf.at[slot], zero_out.at[:, pl.ds(pl.multiple_of(place * 1024 + half * 512, 512), 512)])
            ones.append(dot(zero, pool1).astype(BF))
        one = jnp.concatenate(ones, axis=1)
        one_buf[n] = one
        send(one_buf.at[n], one_out.at[:, pl.ds(pl.multiple_of(place * 256, 256), 256)])
        two = dot(one, pool2).astype(BF)
        three = dot(two, pool3).astype(BF)
        small = jnp.concatenate([two, three], axis=1)
        places.append(place)
        smalls.append(small)
        if not merge and not last:
            small_buf[n] = small
            send(small_buf.at[n], small_out.at[place])
    if merge:
        for m in range(Z):
            piece = small_ref[m]
            for place, small in zip(places, smalls):
                piece = jnp.where(place == m, small, piece)
            two_buf[:, m * 64 : (m + 1) * 64] = piece[:, 0:64]
            three_buf[:, m * 16 : (m + 1) * 16] = piece[:, 64:80]
    if last:
        two_buf[...] = two_ref[...]
        three_buf[...] = three_ref[...]
        for m in range(Z):

            @pl.when(places[0] == m)
            def _():
                two_buf[:, m * 64 : (m + 1) * 64] = smalls[0][:, 0:64]
                three_buf[:, m * 16 : (m + 1) * 16] = smalls[0][:, 64:80]

        send(two_buf, two_out)
        send(three_buf, three_out)
    for copy in copies:
        copy.wait()


def planes_call(offsets, hidden, first, proj_weight, proj_bias, outs, merge=False, last=False):
    count = len(offsets)
    args = [first, proj_weight, proj_bias, *hidden]
    in_specs = [VMEM] * len(args)
    aliases = {}
    if outs is not None:
        shared = 2 if merge or last else 3
        aliases = {len(args) + n: n for n in range(shared)}
        args += list(outs)
        in_specs += [ANYWHERE] * shared + [VMEM] * (len(outs) - shared)
    small = [(512, 512), (512, 128)] if merge or last else [(8, 512, 128)]
    shapes = [(512, 8192), (512, 2048)] + small
    out_specs = [ANYWHERE] * 2 + [VMEM if merge else ANYWHERE] * len(small)
    scratch = [(2 * count, 512, 512), (count, 512, 256)]
    scratch += [] if merge else small + [(8, 128, 128)] if last else [(count, 512, 128)]
    return pl.pallas_call(
        functools.partial(planes_kernel, offsets, merge, last, len(aliases)),
        in_specs=in_specs,
        out_specs=out_specs,
        out_shape=[jax.ShapeDtypeStruct(shape, BF) for shape in shapes],
        scratch_shapes=[pltpu.VMEM(shape, BF) for shape in scratch] + [pltpu.SemaphoreType.DMA((5 * count,))],
        input_output_aliases=aliases,
        compiler_params=pltpu.CompilerParams(vmem_limit_bytes=24 << 20),
        cost_estimate=pl.CostEstimate(
            flops=1_400_000_000 * count, bytes_accessed=1_500_000 * count, transcendentals=0
        ),
        name="planes",
    )(*args)


def per_device(images, conv_weight, conv_bias, proj_weight, proj_bias):
    right = [(c, c + 1) for c in range(COLS - 1)]
    down = [(r, r + 1) for r in range(ROWS - 1)]
    diagonal = [(r * COLS + c, (r + 1) * COLS + c + 1) for r in range(ROWS - 1) for c in range(COLS - 1)]
    main, top, left, corner = split_tile(images)
    params = (conv_weight.T, conv_bias[None, :], proj_weight, proj_bias.reshape(2, 128))
    main, top, left, corner, params = lax.optimization_barrier((main, top, left, corner, params))
    left = lax.ppermute(left, "cols", right)
    top = lax.ppermute(top, "rows", down)
    corner = lax.ppermute(corner, ("rows", "cols"), diagonal)
    conv_weight, conv_bias, proj_weight, proj_bias = stage(*params)
    hidden_one, hidden_two = hidden_of(main, top, left, corner, conv_weight, conv_bias)

    def along(axis, steps):
        size, stride = {"z": (Z, PLANE), "yh": (YH, X), "x": (X, 1)}[axis]
        target = lambda r: r + ((r // stride + steps) % size - (r // stride) % size) * stride
        return [(r, target(r)) for r in range(ROWS)]

    other = lax.ppermute(hidden_two, "rows", along("yh", 1))
    ones = [hidden_one]
    ones += [lax.ppermute(hidden_one, "cols", [(k, k ^ m) for k in range(COLS)]) for m in range(1, 4)]
    other, ones = lax.optimization_barrier((other, ones))
    pair = jnp.stack([hidden_two, other])
    mine = jnp.concatenate([pair] + [lax.ppermute(pair, "rows", along("x", -s)) for s in range(1, X)])
    first = feats_one(ones, proj_weight, proj_bias)

    call = functools.partial(planes_call, first=first, proj_weight=proj_weight, proj_bias=proj_bias)
    below, above = mine, mine
    outs = call((0,), [mine], outs=None)
    for step in range(1, Z // 2):
        below = lax.ppermute(below, "rows", along("z", 1))
        above = lax.ppermute(above, "rows", along("z", -1))
        outs = call((-step, step), [below, above], outs=outs, merge=step == Z // 2 - 1)
    below = lax.ppermute(below[:4], "rows", along("z", 1))
    above = lax.ppermute(above[4:], "rows", along("z", -1))
    return tuple(call((Z // 2,), [below, above], outs=outs, last=True))


def solution(mesh):
    in_specs = (P(None, None, "rows", "cols"), P(), P(), P(), P())
    out_specs = (P("rows", "cols"), P("rows", "cols"), P("rows", "cols"), P("rows", "cols"))
    return jax.shard_map(
        per_device, mesh=mesh, in_specs=in_specs, out_specs=out_specs, check_vma=False
    )
```

```python
import functools

import jax
import jax.numpy as jnp
from jax import lax
from jax.experimental import pallas as pl
from jax.experimental.pallas import tpu as pltpu
from jax.sharding import PartitionSpec as P

Z, YH, X = 8, 2, 4
PLANE = YH * X
ROWS, COLS = Z * PLANE, 4
BF, F32 = jnp.bfloat16, jnp.float32


def dot(a, b):
    return jnp.dot(a, b, preferred_element_type=F32)


def dot_nt(a, b):
    return lax.dot_general(a, b, (((1,), (1,)), ((), ())), preferred_element_type=F32)


def dot_tn(a, b):
    return lax.dot_general(a, b, (((0,), (0,)), ((), ())), preferred_element_type=F32)


def iotas(*shape):
    return lax.broadcasted_iota(jnp.int32, shape, 0), lax.broadcasted_iota(jnp.int32, shape, 1)


def position():
    r = lax.axis_index("rows")
    return r // PLANE, r // X % YH, r % X


VMEM, SMEM = pl.BlockSpec(memory_space=pltpu.VMEM), pl.BlockSpec(memory_space=pltpu.SMEM)
ANYWHERE = pl.BlockSpec(memory_space=pl.ANY)
SMALL = pltpu.CompilerParams(vmem_limit_bytes=12 << 20)


def one_hot(mask, value=1.0):
    return jnp.where(mask, value, 0.0).astype(BF)


def stage_kernel(*refs):
    count = len(refs) // 2
    for n in range(count):
        refs[count + n][...] = refs[n][...]


def stage(*params):
    return pl.pallas_call(
        stage_kernel,
        out_shape=[jax.ShapeDtypeStruct(param.shape, param.dtype) for param in params],
        compiler_params=SMALL,
        cost_estimate=pl.CostEstimate(flops=1_000_000_000, bytes_accessed=600_000, transcendentals=0),
        name="stage",
    )(*params)


def split_kernel(tile_ref, main_ref, top_ref, left_ref, corner_ref):
    row, col = iotas(384, 384)
    tap = (row >= 96).astype(jnp.int32) + (row >= 192).astype(jnp.int32) + (row >= 288).astype(jnp.int32)
    order = one_hot(col == (row - 96 * tap) * 4 + tap)
    row, col = iotas(16, 256)
    rim = one_hot((row < 2) & (col == row * 128 + 127))
    main = dot(order, jnp.concatenate([tile_ref[0], tile_ref[1]], axis=1)).astype(BF)
    main_ref[...] = main
    top_ref[...] = main[288:384]
    left_ref[...] = dot_nt(rim, main).astype(BF)
    corner_ref[...] = dot_nt(rim, main[288:384]).astype(BF)


def split_tile(images):
    return pl.pallas_call(
        split_kernel,
        out_shape=[jax.ShapeDtypeStruct(shape, BF) for shape in ((384, 256), (96, 256), (16, 384), (16, 96))],
        compiler_params=SMALL,
        name="split_tile",
    )(images.reshape(2, 384, 128))


def hidden_kernel(main_ref, top_ref, left_ref, corner_ref, weight_ref, bias_ref, one_ref, two_ref):
    rows = jnp.concatenate([top_ref[...], main_ref[...]], axis=0)
    row, col = iotas(256, 384)
    source = 2 * (col & 63) - 1 + (col >> 7) + jnp.where((col & 64) != 0, 128, 0)
    valid = ((col & 63) != 0) | (col >= 128)
    taps = dot(rows, one_hot((row == source) & valid))
    row, col = iotas(16, 128)
    place = one_hot((row < 2) & (col == row * 64))
    rim = jnp.concatenate([dot_tn(corner_ref[...], place), dot_tn(left_ref[...], place)], axis=0)
    first = (taps[:, :128] + rim).astype(BF)
    parts = [first, taps[:, 128:256].astype(BF), taps[:, 256:384].astype(BF)]
    stacked = jnp.concatenate(
        [
            jnp.concatenate(
                [parts[b][(2 * i + a) * 96 : (2 * i + a + 1) * 96] for a in range(3) for b in range(3)], axis=0
            )
            for i in range(2)
        ],
        axis=1,
    )
    pre = dot_tn(weight_ref[...], stacked)
    bias = jnp.transpose(jnp.broadcast_to(bias_ref[...], (128, 128)))
    hidden = [jnp.maximum(pre[:, i * 128 : (i + 1) * 128] + bias, 0.0) for i in range(2)]
    lane = lax.broadcasted_iota(jnp.int32, (128, 128), 1)
    one_ref[...] = jnp.where(lane < 64, hidden[0], pltpu.roll(hidden[1], 64, 1)).astype(BF)
    two_ref[...] = jnp.where(lane < 64, pltpu.roll(hidden[0], 64, 1), hidden[1]).astype(BF)


def hidden_of(main, top, left, corner, conv_weight, conv_bias):
    return pl.pallas_call(
        hidden_kernel,
        out_shape=[jax.ShapeDtypeStruct((128, 128), BF)] * 2,
        compiler_params=SMALL,
        name="hidden",
    )(main, top, left, corner, conv_weight, conv_bias)


def feats_one_kernel(own_ref, swapped_ref, far_ref, weight_ref, bias_ref, out_ref):
    hidden = [own_ref[...], swapped_ref[...], far_ref[0], far_ref[1]]
    for m in range(4):
        k = lax.axis_index("cols") ^ m
        feats = lax.dot_general(
            hidden[m], weight_ref[...], (((0,), (1,)), ((), ())), preferred_element_type=F32
        )
        bias = jnp.concatenate([bias_ref[0:1, :], bias_ref[1:2, :]], axis=1)
        feats = (feats + bias).astype(BF) * jnp.bfloat16(0.0625)
        for i in range(2):
            out_ref[pl.ds(pl.multiple_of(i * 256 + k * 64, 64), 64), :] = feats[i * 64 : (i + 1) * 64, :]


def feats_one(hidden, proj_weight, proj_bias):
    return pl.pallas_call(
        feats_one_kernel,
        out_shape=jax.ShapeDtypeStruct((512, 256), BF),
        compiler_params=SMALL,
        name="feats_one",
    )(*hidden, proj_weight, proj_bias)


def planes_kernel(offsets, last, n_alias, first_ref, weight_ref, bias_ref, *refs):
    n_hid = 2 if last else len(offsets)
    hid_refs, rest = refs[:n_hid], refs[n_hid + n_alias :]
    if last:
        small_ref, zero_out, one_out, two_out, three_out = rest[:5]
        zero_buf, one_buf, two_buf, three_buf, hid_buf, sems = rest[5:]
    else:
        zero_out, one_out, small_out, zero_buf, one_buf, small_buf, sems = rest
    z, yh, x = position()
    order = [((j % X - x) & (X - 1)) * 2 + (yh ^ (j // X)) for j in range(PLANE)]
    row, col = iotas(512, 128)
    pool1 = one_hot(col == (row >> 7) * 32 + ((row & 63) >> 1), 0.25)
    bias = jnp.concatenate(
        [jnp.transpose(jnp.broadcast_to(bias_ref[n : n + 1, :], (128, 128))) for n in range(2)], axis=0
    )
    bias = jnp.concatenate([bias] * 4, axis=1)
    copies = []

    def send(source, target):
        copies.append(pltpu.make_async_copy(source, target, sems.at[len(copies)]))
        copies[-1].start()

    for n, offset in enumerate(offsets):
        place = (z + (offset + Z)) & (Z - 1)
        if last:
            hid_buf[0:4] = hid_refs[0][...]
            hid_buf[4:8] = hid_refs[1][...]
            hid_ref = hid_buf
        else:
            hid_ref = hid_refs[n]
        ones = []
        for half in range(2):
            hid = jnp.concatenate([hid_ref[order[4 * half + j]] for j in range(4)], axis=1)
            feats = (dot(weight_ref[...], hid) + bias).astype(BF)
            zero = dot(first_ref[...], feats).astype(BF)
            slot = 2 * n + half
            zero_buf[slot] = zero
            send(zero_buf.at[slot], zero_out.at[:, pl.ds(pl.multiple_of(place * 1024 + half * 512, 512), 512)])
            ones.append(dot(zero, pool1).astype(BF))
        one = jnp.concatenate(ones, axis=1)
        one_buf[n] = one
        send(one_buf.at[n], one_out.at[:, pl.ds(pl.multiple_of(place * 256, 256), 256)])
        side = place & 1
        row, col = iotas(256, 128)
        two = dot(one, one_hot(col == side * 64 + (row >> 6) * 16 + ((row & 31) >> 1), 0.25)).astype(BF)
        row, col = iotas(128, 128)
        cell = ((row & 63) >> 5) * 8 + ((row & 15) >> 1)
        three = dot(two, one_hot(((row >> 6) == side) & (col == place * 16 + cell), 0.25)).astype(BF)
        if not last:
            small_buf[n, :, :128] = two
            small_buf[n, :, 128:] = three
            send(small_buf.at[n], small_out.at[place])
    if last:
        for m in range(Z // 2):
            parts = [jnp.where(place == k, two, small_ref[k, :, :128]) for k in (2 * m, 2 * m + 1)]
            two_buf[:, m * 128 : (m + 1) * 128] = parts[0] + parts[1]
        send(two_buf, two_out)
        total = three
        for k in range(Z):
            total = total + jnp.where(place == k, jnp.zeros_like(three), small_ref[k, :, 128:])
        three_buf[...] = total
        send(three_buf, three_out)
    for copy in copies:
        copy.wait()


def planes_call(offsets, hidden, first, proj_weight, proj_bias, outs, last=False):
    count = len(offsets)
    args = [first, proj_weight, proj_bias, *hidden]
    in_specs = [VMEM] * len(args)
    aliases = {}
    if outs is not None:
        shared = 2 if last else 3
        aliases = {len(args) + n: n for n in range(shared)}
        args += list(outs)
        in_specs += [ANYWHERE] * shared + [VMEM] * (len(outs) - shared)
    small = [(512, 512), (512, 128)] if last else [(Z, 512, 256)]
    shapes = [(512, 8192), (512, 2048)] + small
    scratch = [(2 * count, 512, 512), (count, 512, 256)]
    scratch += small + [(8, 128, 128)] if last else [(count, 512, 256)]
    return pl.pallas_call(
        functools.partial(planes_kernel, offsets, last, len(aliases)),
        in_specs=in_specs,
        out_specs=[ANYWHERE] * len(shapes),
        out_shape=[jax.ShapeDtypeStruct(shape, BF) for shape in shapes],
        scratch_shapes=[pltpu.VMEM(shape, BF) for shape in scratch] + [pltpu.SemaphoreType.DMA((5 * count,))],
        input_output_aliases=aliases,
        compiler_params=pltpu.CompilerParams(vmem_limit_bytes=24 << 20),
        cost_estimate=pl.CostEstimate(
            flops=1_400_000_000 * count, bytes_accessed=1_500_000 * count, transcendentals=0
        ),
        name="planes",
    )(*args)


def per_device(images, conv_weight, conv_bias, proj_weight, proj_bias):
    right = [(c, c + 1) for c in range(COLS - 1)]
    down = [(r, r + 1) for r in range(ROWS - 1)]
    diagonal = [(r * COLS + c, (r + 1) * COLS + c + 1) for r in range(ROWS - 1) for c in range(COLS - 1)]
    main, top, left, corner = split_tile(images)
    params = (conv_weight.T, conv_bias[None, :])
    main, top, left, corner, params = lax.optimization_barrier((main, top, left, corner, params))
    top = lax.ppermute(top, "rows", down)
    corner = lax.ppermute(corner, ("rows", "cols"), diagonal)
    left = lax.ppermute(left, "cols", right)
    conv_weight, conv_bias = stage(*params)
    hidden_one, hidden_two = hidden_of(main, top, left, corner, conv_weight, conv_bias)

    def along(axis, steps):
        size, stride = {"z": (Z, PLANE), "yh": (YH, X), "x": (X, 1)}[axis]
        target = lambda r: r + ((r // stride + steps) % size - (r // stride) % size) * stride
        return [(r, target(r)) for r in range(ROWS)]

    params = (proj_weight, proj_bias.reshape(2, 128))
    hidden_one, hidden_two, params = lax.optimization_barrier((hidden_one, hidden_two, params))
    other = lax.ppermute(hidden_two, "rows", along("yh", 1))
    proj_weight, proj_bias = stage(*params)
    swapped = lax.ppermute(hidden_one, "cols", [(k, k ^ 1) for k in range(COLS)])
    other, swapped, proj_weight, proj_bias = lax.optimization_barrier((other, swapped, proj_weight, proj_bias))
    pair = jnp.stack([hidden_two, other])
    far = lax.ppermute(jnp.stack([hidden_one, swapped]), "cols", [(k, k ^ 2) for k in range(COLS)])
    mine = jnp.concatenate([pair] + [lax.ppermute(pair, "rows", along("x", -s)) for s in range(1, X)])
    mine, far = lax.optimization_barrier((mine, far))
    first = feats_one((hidden_one, swapped, far), proj_weight, proj_bias)

    call = functools.partial(planes_call, first=first, proj_weight=proj_weight, proj_bias=proj_bias)
    below, above = mine, mine
    outs = call((0,), [mine], outs=None)
    for step in range(1, Z // 2):
        below = lax.ppermute(below, "rows", along("z", 1))
        above = lax.ppermute(above, "rows", along("z", -1))
        outs = call((-step, step), [below, above], outs=outs)
    below = lax.ppermute(below[:4], "rows", along("z", 1))
    above = lax.ppermute(above[4:], "rows", along("z", -1))
    return tuple(call((Z // 2,), [below, above], outs=outs, last=True))


def solution(mesh):
    in_specs = (P(None, None, "rows", "cols"), P(), P(), P(), P())
    out_specs = (P("rows", "cols"), P("rows", "cols"), P("rows", "cols"), P("rows", "cols"))
    return jax.shard_map(
        per_device, mesh=mesh, in_specs=in_specs, out_specs=out_specs, check_vma=False
    )
```

```python
import functools

import jax
import jax.numpy as jnp
from jax import lax
from jax.experimental import pallas as pl
from jax.experimental.pallas import tpu as pltpu
from jax.sharding import PartitionSpec as P

Z, YH, X = 8, 2, 4
PLANE = YH * X
ROWS, COLS = Z * PLANE, 4
BF, F32 = jnp.bfloat16, jnp.float32


def dot(a, b):
    return jnp.dot(a, b, preferred_element_type=F32)


def dot_nt(a, b):
    return lax.dot_general(a, b, (((1,), (1,)), ((), ())), preferred_element_type=F32)


def dot_tn(a, b):
    return lax.dot_general(a, b, (((0,), (0,)), ((), ())), preferred_element_type=F32)


def iotas(*shape):
    return lax.broadcasted_iota(jnp.int32, shape, 0), lax.broadcasted_iota(jnp.int32, shape, 1)


def position():
    r = lax.axis_index("rows")
    return r // PLANE, r // X % YH, r % X


VMEM, SMEM = pl.BlockSpec(memory_space=pltpu.VMEM), pl.BlockSpec(memory_space=pltpu.SMEM)
ANYWHERE = pl.BlockSpec(memory_space=pl.ANY)
SMALL = pltpu.CompilerParams(vmem_limit_bytes=12 << 20)


def one_hot(mask, value=1.0):
    return jnp.where(mask, value, 0.0).astype(BF)


def stage_kernel(*refs):
    count = len(refs) // 2
    for n in range(count):
        refs[count + n][...] = refs[n][...]


def stage(*params):
    return pl.pallas_call(
        stage_kernel,
        out_shape=[jax.ShapeDtypeStruct(param.shape, param.dtype) for param in params],
        compiler_params=SMALL,
        cost_estimate=pl.CostEstimate(flops=1_000_000_000, bytes_accessed=600_000, transcendentals=0),
        name="stage",
    )(*params)


def split_kernel(tile_ref, main_ref, top_ref, left_ref):
    row, col = iotas(384, 384)
    tap = (row >= 96).astype(jnp.int32) + (row >= 192).astype(jnp.int32) + (row >= 288).astype(jnp.int32)
    order = one_hot(col == (row - 96 * tap) * 4 + tap)
    row, col = iotas(16, 256)
    rim = one_hot((row < 2) & (col == row * 128 + 127))
    main = dot(order, jnp.concatenate([tile_ref[0], tile_ref[1]], axis=1)).astype(BF)
    main_ref[...] = main
    top_ref[...] = main[288:384]
    left_ref[...] = dot_nt(rim, main).astype(BF)


def split_tile(images):
    return pl.pallas_call(
        split_kernel,
        out_shape=[jax.ShapeDtypeStruct(shape, BF) for shape in ((384, 256), (96, 256), (16, 384))],
        compiler_params=SMALL,
        name="split_tile",
    )(images.reshape(2, 384, 128))


def hidden_kernel(main_ref, top_ref, left_ref, corner_ref, weight_ref, bias_ref, one_ref, two_ref):
    rows = jnp.concatenate([top_ref[...], main_ref[...]], axis=0)
    row, col = iotas(256, 384)
    source = 2 * (col & 63) - 1 + (col >> 7) + jnp.where((col & 64) != 0, 128, 0)
    valid = ((col & 63) != 0) | (col >= 128)
    taps = dot(rows, one_hot((row == source) & valid))
    row, col = iotas(16, 128)
    place = one_hot((row < 2) & (col == row * 64))
    row, col = iotas(256, 128)
    last = one_hot(((row & 127) == 127) & (col == (row >> 7) * 64))
    rim = jnp.concatenate([dot(corner_ref[...], last), dot_tn(left_ref[...], place)], axis=0)
    first = (taps[:, :128] + rim).astype(BF)
    parts = [first, taps[:, 128:256].astype(BF), taps[:, 256:384].astype(BF)]
    stacked = jnp.concatenate(
        [
            jnp.concatenate(
                [parts[b][(2 * i + a) * 96 : (2 * i + a + 1) * 96] for a in range(3) for b in range(3)], axis=0
            )
            for i in range(2)
        ],
        axis=1,
    )
    pre = dot_tn(weight_ref[...], stacked)
    bias = jnp.transpose(jnp.broadcast_to(bias_ref[...], (128, 128)))
    hidden = [jnp.maximum(pre[:, i * 128 : (i + 1) * 128] + bias, 0.0) for i in range(2)]
    lane = lax.broadcasted_iota(jnp.int32, (128, 128), 1)
    one_ref[...] = jnp.where(lane < 64, hidden[0], pltpu.roll(hidden[1], 64, 1)).astype(BF)
    two_ref[...] = jnp.where(lane < 64, pltpu.roll(hidden[0], 64, 1), hidden[1]).astype(BF)


def hidden_of(main, top, left, corner, conv_weight, conv_bias):
    return pl.pallas_call(
        hidden_kernel,
        out_shape=[jax.ShapeDtypeStruct((128, 128), BF)] * 2,
        compiler_params=SMALL,
        name="hidden",
    )(main, top, left, corner, conv_weight, conv_bias)


def feats_one_kernel(own_ref, swapped_ref, far_ref, weight_ref, bias_ref, out_ref):
    hidden = [own_ref[...], swapped_ref[...], far_ref[0], far_ref[1]]
    for m in range(4):
        k = lax.axis_index("cols") ^ m
        feats = lax.dot_general(
            hidden[m], weight_ref[...], (((0,), (1,)), ((), ())), preferred_element_type=F32
        )
        bias = jnp.concatenate([bias_ref[0:1, :], bias_ref[1:2, :]], axis=1)
        feats = (feats + bias).astype(BF) * jnp.bfloat16(0.0625)
        for i in range(2):
            out_ref[pl.ds(pl.multiple_of(i * 256 + k * 64, 64), 64), :] = feats[i * 64 : (i + 1) * 64, :]


def feats_one(hidden, proj_weight, proj_bias):
    return pl.pallas_call(
        feats_one_kernel,
        out_shape=jax.ShapeDtypeStruct((512, 256), BF),
        compiler_params=SMALL,
        name="feats_one",
    )(*hidden, proj_weight, proj_bias)


def planes_kernel(offsets, last, n_alias, first_ref, weight_ref, bias_ref, *refs):
    n_hid = 2 if last else len(offsets)
    hid_refs, rest = refs[:n_hid], refs[n_hid + n_alias :]
    if last:
        small_ref, zero_out, one_out, two_out, three_out = rest[:5]
        zero_buf, one_buf, two_buf, three_buf, hid_buf, sems = rest[5:]
    else:
        zero_out, one_out, small_out, zero_buf, one_buf, small_buf, sems = rest
    z, yh, x = position()
    order = [((j % X - x) & (X - 1)) * 2 + (yh ^ (j // X)) for j in range(PLANE)]
    row, col = iotas(512, 128)
    pool1 = one_hot(col == (row >> 7) * 32 + ((row & 63) >> 1), 0.25)
    bias = jnp.concatenate(
        [jnp.transpose(jnp.broadcast_to(bias_ref[n : n + 1, :], (128, 128))) for n in range(2)], axis=0
    )
    bias = jnp.concatenate([bias] * 4, axis=1)
    copies = []

    def send(source, target):
        copies.append(pltpu.make_async_copy(source, target, sems.at[len(copies)]))
        copies[-1].start()

    for n, offset in enumerate(offsets):
        place = (z + (offset + Z)) & (Z - 1)
        if last:
            hid_buf[0:4] = hid_refs[0][...]
            hid_buf[4:8] = hid_refs[1][...]
            hid_ref = hid_buf
        else:
            hid_ref = hid_refs[n]
        ones = []
        for half in range(2):
            hid = jnp.concatenate([hid_ref[order[4 * half + j]] for j in range(4)], axis=1)
            feats = (dot(weight_ref[...], hid) + bias).astype(BF)
            zero = dot(first_ref[...], feats).astype(BF)
            slot = 2 * n + half
            zero_buf[slot] = zero
            send(zero_buf.at[slot], zero_out.at[:, pl.ds(pl.multiple_of(place * 1024 + half * 512, 512), 512)])
            ones.append(dot(zero, pool1).astype(BF))
        one = jnp.concatenate(ones, axis=1)
        one_buf[n] = one
        send(one_buf.at[n], one_out.at[:, pl.ds(pl.multiple_of(place * 256, 256), 256)])
        side = place & 1
        row, col = iotas(256, 128)
        two = dot(one, one_hot(col == side * 64 + (row >> 6) * 16 + ((row & 31) >> 1), 0.25)).astype(BF)
        row, col = iotas(128, 128)
        cell = ((row & 63) >> 5) * 8 + ((row & 15) >> 1)
        three = dot(two, one_hot(((row >> 6) == side) & (col == place * 16 + cell), 0.25)).astype(BF)
        if not last:
            small_buf[n, :, :128] = two
            small_buf[n, :, 128:] = three
            send(small_buf.at[n], small_out.at[place])
    if last:
        for m in range(Z // 2):
            parts = [jnp.where(place == k, two, small_ref[k, :, :128]) for k in (2 * m, 2 * m + 1)]
            two_buf[:, m * 128 : (m + 1) * 128] = parts[0] + parts[1]
        send(two_buf, two_out)
        total = three
        for k in range(Z):
            total = total + jnp.where(place == k, jnp.zeros_like(three), small_ref[k, :, 128:])
        three_buf[...] = total
        send(three_buf, three_out)
    for copy in copies:
        copy.wait()


def planes_call(offsets, hidden, first, proj_weight, proj_bias, outs, last=False):
    count = len(offsets)
    args = [first, proj_weight, proj_bias, *hidden]
    in_specs = [VMEM] * len(args)
    aliases = {}
    if outs is not None:
        shared = 2 if last else 3
        aliases = {len(args) + n: n for n in range(shared)}
        args += list(outs)
        in_specs += [ANYWHERE] * shared + [VMEM] * (len(outs) - shared)
    small = [(512, 512), (512, 128)] if last else [(Z, 512, 256)]
    shapes = [(512, 8192), (512, 2048)] + small
    scratch = [(2 * count, 512, 512), (count, 512, 256)]
    scratch += small + [(8, 128, 128)] if last else [(count, 512, 256)]
    return pl.pallas_call(
        functools.partial(planes_kernel, offsets, last, len(aliases)),
        in_specs=in_specs,
        out_specs=[ANYWHERE] * len(shapes),
        out_shape=[jax.ShapeDtypeStruct(shape, BF) for shape in shapes],
        scratch_shapes=[pltpu.VMEM(shape, BF) for shape in scratch] + [pltpu.SemaphoreType.DMA((5 * count,))],
        input_output_aliases=aliases,
        compiler_params=pltpu.CompilerParams(vmem_limit_bytes=24 << 20),
        cost_estimate=pl.CostEstimate(
            flops=1_400_000_000 * count, bytes_accessed=1_500_000 * count, transcendentals=0
        ),
        name="planes",
    )(*args)


def per_device(images, conv_weight, conv_bias, proj_weight, proj_bias):
    right = [(c, c + 1) for c in range(COLS - 1)]
    down = [(r, r + 1) for r in range(ROWS - 1)]
    diagonal = [(r * COLS + c, (r + 1) * COLS + c + 1) for r in range(ROWS - 1) for c in range(COLS - 1)]
    main, top, left = split_tile(images)
    params = (conv_weight.T, conv_bias[None, :])
    main, top, left, params = lax.optimization_barrier((main, top, left, params))
    corner = lax.ppermute(top, ("rows", "cols"), diagonal)
    top = lax.ppermute(top, "rows", down)
    left = lax.ppermute(left, "cols", right)
    conv_weight, conv_bias = stage(*params)
    hidden_one, hidden_two = hidden_of(main, top, left, corner, conv_weight, conv_bias)

    def along(axis, steps):
        size, stride = {"z": (Z, PLANE), "yh": (YH, X), "x": (X, 1)}[axis]
        target = lambda r: r + ((r // stride + steps) % size - (r // stride) % size) * stride
        return [(r, target(r)) for r in range(ROWS)]

    params = (proj_weight, proj_bias.reshape(2, 128))
    hidden_one, hidden_two, params = lax.optimization_barrier((hidden_one, hidden_two, params))
    other = lax.ppermute(hidden_two, "rows", along("yh", 1))
    proj_weight, proj_bias = stage(*params)
    swapped = lax.ppermute(hidden_one, "cols", [(k, k ^ 1) for k in range(COLS)])
    other, swapped, proj_weight, proj_bias = lax.optimization_barrier((other, swapped, proj_weight, proj_bias))
    pair = jnp.stack([hidden_two, other])
    far = lax.ppermute(jnp.stack([hidden_one, swapped]), "cols", [(k, k ^ 2) for k in range(COLS)])
    mine = jnp.concatenate([pair] + [lax.ppermute(pair, "rows", along("x", -s)) for s in range(1, X)])
    mine, far = lax.optimization_barrier((mine, far))
    first = feats_one((hidden_one, swapped, far), proj_weight, proj_bias)

    call = functools.partial(planes_call, first=first, proj_weight=proj_weight, proj_bias=proj_bias)
    below, above = mine, mine
    outs = call((0,), [mine], outs=None)
    for step in range(1, Z // 2):
        below = lax.ppermute(below, "rows", along("z", 1))
        above = lax.ppermute(above, "rows", along("z", -1))
        outs = call((-step, step), [below, above], outs=outs)
    below = lax.ppermute(below[:4], "rows", along("z", 1))
    above = lax.ppermute(above[4:], "rows", along("z", -1))
    return tuple(call((Z // 2,), [below, above], outs=outs, last=True))


def solution(mesh):
    in_specs = (P(None, None, "rows", "cols"), P(), P(), P(), P())
    out_specs = (P("rows", "cols"), P("rows", "cols"), P("rows", "cols"), P("rows", "cols"))
    return jax.shard_map(
        per_device, mesh=mesh, in_specs=in_specs, out_specs=out_specs, check_vma=False
    )
```

```python
import functools

import jax
import jax.numpy as jnp
from jax import lax
from jax.experimental import pallas as pl
from jax.experimental.pallas import tpu as pltpu
from jax.sharding import PartitionSpec as P

Z, YH, X = 8, 2, 4
PLANE = YH * X
ROWS, COLS = Z * PLANE, 4
BF, F32 = jnp.bfloat16, jnp.float32


def dot(a, b):
    return jnp.dot(a, b, preferred_element_type=F32)


def dot_nt(a, b):
    return lax.dot_general(a, b, (((1,), (1,)), ((), ())), preferred_element_type=F32)


def dot_tn(a, b):
    return lax.dot_general(a, b, (((0,), (0,)), ((), ())), preferred_element_type=F32)


def iotas(*shape):
    return lax.broadcasted_iota(jnp.int32, shape, 0), lax.broadcasted_iota(jnp.int32, shape, 1)


def position():
    r = lax.axis_index("rows")
    return r // PLANE, r // X % YH, r % X


VMEM, SMEM = pl.BlockSpec(memory_space=pltpu.VMEM), pl.BlockSpec(memory_space=pltpu.SMEM)
ANYWHERE = pl.BlockSpec(memory_space=pl.ANY)
SMALL = pltpu.CompilerParams(vmem_limit_bytes=12 << 20)


def one_hot(mask, value=1.0):
    return jnp.where(mask, value, 0.0).astype(BF)


def stage_kernel(*refs):
    count = len(refs) // 2
    for n in range(count):
        refs[count + n][...] = refs[n][...]


def stage(*params):
    return pl.pallas_call(
        stage_kernel,
        out_shape=[jax.ShapeDtypeStruct(param.shape, param.dtype) for param in params],
        compiler_params=SMALL,
        cost_estimate=pl.CostEstimate(flops=1_000_000_000, bytes_accessed=600_000, transcendentals=0),
        name="stage",
    )(*params)


def split_kernel(tile_ref, main_ref, top_ref, left_ref):
    row, col = iotas(384, 384)
    tap = (row >= 96).astype(jnp.int32) + (row >= 192).astype(jnp.int32) + (row >= 288).astype(jnp.int32)
    order = one_hot(col == (row - 96 * tap) * 4 + tap)
    row, col = iotas(16, 256)
    rim = one_hot((row < 2) & (col == row * 128 + 127))
    main = dot(order, jnp.concatenate([tile_ref[0], tile_ref[1]], axis=1)).astype(BF)
    main_ref[...] = main
    top_ref[...] = main[288:384]
    left_ref[...] = dot_nt(rim, main).astype(BF)


def split_tile(images):
    return pl.pallas_call(
        split_kernel,
        out_shape=[jax.ShapeDtypeStruct(shape, BF) for shape in ((384, 256), (96, 256), (16, 384))],
        compiler_params=SMALL,
        name="split_tile",
    )(images.reshape(2, 384, 128))


def hidden_kernel(main_ref, top_ref, left_ref, corner_ref, weight_ref, bias_ref, one_ref, two_ref):
    rows = jnp.concatenate([top_ref[...], main_ref[...]], axis=0)
    row, col = iotas(256, 384)
    source = 2 * (col & 63) - 1 + (col >> 7) + jnp.where((col & 64) != 0, 128, 0)
    valid = ((col & 63) != 0) | (col >= 128)
    taps = dot(rows, one_hot((row == source) & valid))
    row, col = iotas(16, 128)
    place = one_hot((row < 2) & (col == row * 64))
    row, col = iotas(256, 128)
    last = one_hot(((row & 127) == 127) & (col == (row >> 7) * 64))
    rim = jnp.concatenate([dot(corner_ref[...], last), dot_tn(left_ref[...], place)], axis=0)
    first = (taps[:, :128] + rim).astype(BF)
    parts = [first, taps[:, 128:256].astype(BF), taps[:, 256:384].astype(BF)]
    stacked = jnp.concatenate(
        [
            jnp.concatenate(
                [parts[b][(2 * i + a) * 96 : (2 * i + a + 1) * 96] for a in range(3) for b in range(3)], axis=0
            )
            for i in range(2)
        ],
        axis=1,
    )
    pre = dot_tn(weight_ref[...], stacked)
    bias = jnp.transpose(jnp.broadcast_to(bias_ref[...], (128, 128)))
    hidden = [jnp.maximum(pre[:, i * 128 : (i + 1) * 128] + bias, 0.0) for i in range(2)]
    lane = lax.broadcasted_iota(jnp.int32, (128, 128), 1)
    one_ref[...] = jnp.where(lane < 64, hidden[0], pltpu.roll(hidden[1], 64, 1)).astype(BF)
    two_ref[...] = jnp.where(lane < 64, pltpu.roll(hidden[0], 64, 1), hidden[1]).astype(BF)


def hidden_of(main, top, left, corner, conv_weight, conv_bias):
    return pl.pallas_call(
        hidden_kernel,
        out_shape=[jax.ShapeDtypeStruct((128, 128), BF)] * 2,
        compiler_params=SMALL,
        name="hidden",
    )(main, top, left, corner, conv_weight, conv_bias)


def feats_one_kernel(own_ref, swapped_ref, far_ref, weight_ref, bias_ref, out_ref):
    hidden = [own_ref[...], swapped_ref[...], far_ref[0], far_ref[1]]
    for m in range(4):
        k = lax.axis_index("cols") ^ m
        feats = lax.dot_general(
            hidden[m], weight_ref[...], (((0,), (1,)), ((), ())), preferred_element_type=F32
        )
        bias = jnp.concatenate([bias_ref[0:1, :], bias_ref[1:2, :]], axis=1)
        feats = (feats + bias).astype(BF) * jnp.bfloat16(0.0625)
        for i in range(2):
            out_ref[pl.ds(pl.multiple_of(i * 256 + k * 64, 64), 64), :] = feats[i * 64 : (i + 1) * 64, :]


def feats_one(hidden, proj_weight, proj_bias):
    return pl.pallas_call(
        feats_one_kernel,
        out_shape=jax.ShapeDtypeStruct((512, 256), BF),
        compiler_params=SMALL,
        name="feats_one",
    )(*hidden, proj_weight, proj_bias)


def pool_one():
    row, col = iotas(512, 128)
    return one_hot(col == (row >> 7) * 32 + ((row & 63) >> 1), 0.25)


def bias_lanes(bias_ref):
    bias = jnp.concatenate(
        [jnp.transpose(jnp.broadcast_to(bias_ref[n : n + 1, :], (128, 128))) for n in range(2)], axis=0
    )
    return jnp.concatenate([bias] * 4, axis=1)


def half_kernel(first_ref, weight_ref, bias_ref, hid_ref, _, zero_out, part_ref, zero_buf, sem):
    z, yh, x = position()
    start = ((z + Z // 2) & (Z - 1)) * 1024 + yh * 512
    hid = jnp.concatenate([hid_ref[(j - x) & (X - 1)] for j in range(X)], axis=1)
    feats = (dot(weight_ref[...], hid) + bias_lanes(bias_ref)).astype(BF)
    zero = dot(first_ref[...], feats).astype(BF)
    zero_buf[...] = zero
    copy = pltpu.make_async_copy(zero_buf, zero_out.at[:, pl.ds(pl.multiple_of(start, 512), 512)], sem)
    copy.start()
    part_ref[...] = dot(zero, pool_one()).astype(BF)
    copy.wait()


def half_call(hidden, first, proj_weight, proj_bias, zero):
    return pl.pallas_call(
        half_kernel,
        in_specs=[VMEM] * 4 + [ANYWHERE],
        out_specs=[ANYWHERE, VMEM],
        out_shape=[jax.ShapeDtypeStruct((512, 8192), BF), jax.ShapeDtypeStruct((512, 128), BF)],
        scratch_shapes=[pltpu.VMEM((512, 512), BF), pltpu.SemaphoreType.DMA],
        input_output_aliases={4: 0},
        compiler_params=SMALL,
        cost_estimate=pl.CostEstimate(flops=700_000_000, bytes_accessed=750_000, transcendentals=0),
        name="half_plane",
    )(first, proj_weight, proj_bias, hidden, zero)


def planes_kernel(offsets, last, n_alias, first_ref, weight_ref, bias_ref, *refs):
    n_hid = len(offsets)
    hid_refs, rest = refs[:n_hid], refs[n_hid + n_alias :]
    if last:
        small_ref, part_ref, zero_out, one_out, two_out, three_out = rest[:6]
        zero_buf, one_buf, two_buf, three_buf, sems = rest[6:]
    else:
        zero_out, one_out, small_out, zero_buf, one_buf, small_buf, sems = rest
    z, yh, x = position()
    order = [(yh ^ (j // X)) * X + ((j % X - x) & (X - 1)) for j in range(PLANE)]
    pool1, bias = pool_one(), bias_lanes(bias_ref)
    copies = []

    def send(source, target):
        copies.append(pltpu.make_async_copy(source, target, sems.at[len(copies)]))
        copies[-1].start()

    for n, offset in enumerate(offsets):
        place = (z + (offset + Z)) & (Z - 1)
        hid_ref = hid_refs[n]
        ones = []
        for half in (1 - yh,) if last else (0, 1):
            blocks = order[:X] if last else order[X * half : X * (half + 1)]
            hid = jnp.concatenate([hid_ref[block & (X - 1) if last else block] for block in blocks], axis=1)
            feats = (dot(weight_ref[...], hid) + bias).astype(BF)
            zero = dot(first_ref[...], feats).astype(BF)
            slot = 2 * n + len(ones)
            zero_buf[slot] = zero
            send(zero_buf.at[slot], zero_out.at[:, pl.ds(pl.multiple_of(place * 1024 + half * 512, 512), 512)])
            ones.append(dot(zero, pool1).astype(BF))
        if last:
            part = part_ref[...]
            ones = [jnp.where(yh == 0, part, ones[0]), jnp.where(yh == 0, ones[0], part)]
        one = jnp.concatenate(ones, axis=1)
        one_buf[n] = one
        send(one_buf.at[n], one_out.at[:, pl.ds(pl.multiple_of(place * 256, 256), 256)])
        side = place & 1
        row, col = iotas(256, 128)
        two = dot(one, one_hot(col == side * 64 + (row >> 6) * 16 + ((row & 31) >> 1), 0.25)).astype(BF)
        row, col = iotas(128, 128)
        cell = ((row & 63) >> 5) * 8 + ((row & 15) >> 1)
        three = dot(two, one_hot(((row >> 6) == side) & (col == place * 16 + cell), 0.25)).astype(BF)
        if not last:
            small_buf[n, :, :128] = two
            small_buf[n, :, 128:] = three
            send(small_buf.at[n], small_out.at[place])
    if last:
        for m in range(Z // 2):
            parts = [jnp.where(place == k, two, small_ref[k, :, :128]) for k in (2 * m, 2 * m + 1)]
            two_buf[:, m * 128 : (m + 1) * 128] = parts[0] + parts[1]
        send(two_buf, two_out)
        total = three
        for k in range(Z):
            total = total + jnp.where(place == k, jnp.zeros_like(three), small_ref[k, :, 128:])
        three_buf[...] = total
        send(three_buf, three_out)
    for copy in copies:
        copy.wait()


def planes_call(offsets, hidden, first, proj_weight, proj_bias, outs, last=False):
    count = len(offsets)
    args = [first, proj_weight, proj_bias, *hidden]
    in_specs = [VMEM] * len(args)
    aliases = {}
    if outs is not None:
        shared = 2 if last else 3
        aliases = {len(args) + n: n for n in range(shared)}
        args += list(outs)
        in_specs += [ANYWHERE] * shared + [VMEM] * (len(outs) - shared)
    small = [(512, 512), (512, 128)] if last else [(Z, 512, 256)]
    shapes = [(512, 8192), (512, 2048)] + small
    scratch = [(2 * count, 512, 512), (count, 512, 256)]
    scratch += small if last else [(count, 512, 256)]
    return pl.pallas_call(
        functools.partial(planes_kernel, offsets, last, len(aliases)),
        in_specs=in_specs,
        out_specs=[ANYWHERE] * len(shapes),
        out_shape=[jax.ShapeDtypeStruct(shape, BF) for shape in shapes],
        scratch_shapes=[pltpu.VMEM(shape, BF) for shape in scratch] + [pltpu.SemaphoreType.DMA((5 * count,))],
        input_output_aliases=aliases,
        compiler_params=pltpu.CompilerParams(vmem_limit_bytes=24 << 20),
        cost_estimate=pl.CostEstimate(
            flops=1_400_000_000 * count, bytes_accessed=1_500_000 * count, transcendentals=0
        ),
        name="planes",
    )(*args)


def per_device(images, conv_weight, conv_bias, proj_weight, proj_bias):
    right = [(c, c + 1) for c in range(COLS - 1)]
    down = [(r, r + 1) for r in range(ROWS - 1)]
    diagonal = [(r * COLS + c, (r + 1) * COLS + c + 1) for r in range(ROWS - 1) for c in range(COLS - 1)]
    main, top, left = split_tile(images)
    params = (conv_weight.T, conv_bias[None, :])
    main, top, left, params = lax.optimization_barrier((main, top, left, params))
    corner = lax.ppermute(top, ("rows", "cols"), diagonal)
    top = lax.ppermute(top, "rows", down)
    left = lax.ppermute(left, "cols", right)
    conv_weight, conv_bias = stage(*params)
    hidden_one, hidden_two = hidden_of(main, top, left, corner, conv_weight, conv_bias)

    def along(axis, steps):
        size, stride = {"z": (Z, PLANE), "yh": (YH, X), "x": (X, 1)}[axis]
        target = lambda r: r + ((r // stride + steps) % size - (r // stride) % size) * stride
        return [(r, target(r)) for r in range(ROWS)]

    params = (proj_weight, proj_bias.reshape(2, 128))
    hidden_one, hidden_two, params = lax.optimization_barrier((hidden_one, hidden_two, params))
    other = lax.ppermute(hidden_two, "rows", along("yh", 1))
    proj_weight, proj_bias = stage(*params)
    swapped = lax.ppermute(hidden_one, "cols", [(k, k ^ 1) for k in range(COLS)])
    other, swapped, proj_weight, proj_bias = lax.optimization_barrier((other, swapped, proj_weight, proj_bias))
    pair = jnp.stack([hidden_two, other])
    far = lax.ppermute(jnp.stack([hidden_one, swapped]), "cols", [(k, k ^ 2) for k in range(COLS)])
    pairs = [pair] + [lax.ppermute(pair, "rows", along("x", -s)) for s in range(1, X)]
    mine = jnp.concatenate([p[n : n + 1] for n in range(YH) for p in pairs])
    mine, far = lax.optimization_barrier((mine, far))
    first = feats_one((hidden_one, swapped, far), proj_weight, proj_bias)

    call = functools.partial(planes_call, first=first, proj_weight=proj_weight, proj_bias=proj_bias)
    below, above = mine, mine
    outs = call((0,), [mine], outs=None)
    for step in range(1, Z // 2):
        below = lax.ppermute(below, "rows", along("z", 1))
        above = lax.ppermute(above, "rows", along("z", -1))
        outs = call((-step, step), [below, above], outs=outs)
    below = lax.ppermute(below[:4], "rows", along("z", 1))
    above = lax.ppermute(above[4:], "rows", along("z", -1))
    zero, part = half_call(below, first, proj_weight, proj_bias, outs[0])
    return tuple(call((Z // 2,), [above], outs=[zero, outs[1], outs[2], part], last=True))


def solution(mesh):
    in_specs = (P(None, None, "rows", "cols"), P(), P(), P(), P())
    out_specs = (P("rows", "cols"), P("rows", "cols"), P("rows", "cols"), P("rows", "cols"))
    return jax.shard_map(
        per_device, mesh=mesh, in_specs=in_specs, out_specs=out_specs, check_vma=False
    )
```

```python
import functools

import jax
import jax.numpy as jnp
from jax import lax
from jax.experimental import pallas as pl
from jax.experimental.pallas import tpu as pltpu
from jax.sharding import PartitionSpec as P

Z, YH, X = 8, 2, 4
PLANE = YH * X
ROWS, COLS = Z * PLANE, 4
BF, F32 = jnp.bfloat16, jnp.float32


def dot(a, b):
    return jnp.dot(a, b, preferred_element_type=F32)


def dot_nt(a, b):
    return lax.dot_general(a, b, (((1,), (1,)), ((), ())), preferred_element_type=F32)


def dot_tn(a, b):
    return lax.dot_general(a, b, (((0,), (0,)), ((), ())), preferred_element_type=F32)


def iotas(*shape):
    return lax.broadcasted_iota(jnp.int32, shape, 0), lax.broadcasted_iota(jnp.int32, shape, 1)


def position():
    r = lax.axis_index("rows")
    return r // PLANE, r // X % YH, r % X


VMEM, SMEM = pl.BlockSpec(memory_space=pltpu.VMEM), pl.BlockSpec(memory_space=pltpu.SMEM)
ANYWHERE = pl.BlockSpec(memory_space=pl.ANY)
SMALL = pltpu.CompilerParams(vmem_limit_bytes=12 << 20)


def one_hot(mask, value=1.0):
    return jnp.where(mask, value, 0.0).astype(BF)


def stage_kernel(*refs):
    count = len(refs) // 2
    for n in range(count):
        refs[count + n][...] = refs[n][...]


def stage(*params):
    return pl.pallas_call(
        stage_kernel,
        out_shape=[jax.ShapeDtypeStruct(param.shape, param.dtype) for param in params],
        compiler_params=SMALL,
        cost_estimate=pl.CostEstimate(flops=1_000_000_000, bytes_accessed=600_000, transcendentals=0),
        name="stage",
    )(*params)


def split_kernel(tile_ref, main_ref, top_ref, left_ref):
    row, col = iotas(384, 384)
    tap = (row >= 96).astype(jnp.int32) + (row >= 192).astype(jnp.int32) + (row >= 288).astype(jnp.int32)
    order = one_hot(col == (row - 96 * tap) * 4 + tap)
    row, col = iotas(16, 256)
    rim = one_hot((row < 2) & (col == row * 128 + 127))
    main = dot(order, jnp.concatenate([tile_ref[0], tile_ref[1]], axis=1)).astype(BF)
    main_ref[...] = main
    top_ref[...] = main[288:384]
    left_ref[...] = dot_nt(rim, main).astype(BF)


def split_tile(images):
    return pl.pallas_call(
        split_kernel,
        out_shape=[jax.ShapeDtypeStruct(shape, BF) for shape in ((384, 256), (96, 256), (16, 384))],
        compiler_params=SMALL,
        name="split_tile",
    )(images.reshape(2, 384, 128))


def hidden_kernel(main_ref, top_ref, left_ref, corner_ref, weight_ref, bias_ref, one_ref, two_ref):
    rows = jnp.concatenate([top_ref[...], main_ref[...]], axis=0)
    row, col = iotas(256, 384)
    source = 2 * (col & 63) - 1 + (col >> 7) + jnp.where((col & 64) != 0, 128, 0)
    valid = ((col & 63) != 0) | (col >= 128)
    taps = dot(rows, one_hot((row == source) & valid))
    row, col = iotas(16, 128)
    place = one_hot((row < 2) & (col == row * 64))
    row, col = iotas(256, 128)
    last = one_hot(((row & 127) == 127) & (col == (row >> 7) * 64))
    rim = jnp.concatenate([dot(corner_ref[...], last), dot_tn(left_ref[...], place)], axis=0)
    first = (taps[:, :128] + rim).astype(BF)
    parts = [first, taps[:, 128:256].astype(BF), taps[:, 256:384].astype(BF)]
    stacked = jnp.concatenate(
        [
            jnp.concatenate(
                [parts[b][(2 * i + a) * 96 : (2 * i + a + 1) * 96] for a in range(3) for b in range(3)], axis=0
            )
            for i in range(2)
        ],
        axis=1,
    )
    pre = dot_tn(weight_ref[...], stacked)
    bias = jnp.transpose(jnp.broadcast_to(bias_ref[...], (128, 128)))
    hidden = [jnp.maximum(pre[:, i * 128 : (i + 1) * 128] + bias, 0.0) for i in range(2)]
    lane = lax.broadcasted_iota(jnp.int32, (128, 128), 1)
    one_ref[...] = jnp.where(lane < 64, hidden[0], pltpu.roll(hidden[1], 64, 1)).astype(BF)
    two_ref[...] = jnp.where(lane < 64, pltpu.roll(hidden[0], 64, 1), hidden[1]).astype(BF)


def hidden_of(main, top, left, corner, conv_weight, conv_bias):
    return pl.pallas_call(
        hidden_kernel,
        out_shape=[jax.ShapeDtypeStruct((128, 128), BF)] * 2,
        compiler_params=SMALL,
        name="hidden",
    )(main, top, left, corner, conv_weight, conv_bias)


def feats_one_kernel(own_ref, swapped_ref, far_ref, weight_ref, bias_ref, out_ref):
    hidden = [own_ref[...], swapped_ref[...], far_ref[0], far_ref[1]]
    for m in range(4):
        k = lax.axis_index("cols") ^ m
        feats = lax.dot_general(
            hidden[m], weight_ref[...], (((0,), (1,)), ((), ())), preferred_element_type=F32
        )
        bias = jnp.concatenate([bias_ref[0:1, :], bias_ref[1:2, :]], axis=1)
        feats = (feats + bias).astype(BF) * jnp.bfloat16(0.0625)
        for i in range(2):
            out_ref[pl.ds(pl.multiple_of(i * 256 + k * 64, 64), 64), :] = feats[i * 64 : (i + 1) * 64, :]


def feats_one(hidden, proj_weight, proj_bias):
    return pl.pallas_call(
        feats_one_kernel,
        out_shape=jax.ShapeDtypeStruct((512, 256), BF),
        compiler_params=SMALL,
        name="feats_one",
    )(*hidden, proj_weight, proj_bias)


def planes_kernel(offsets, last, n_alias, first_ref, weight_ref, bias_ref, *refs):
    n_hid = 2 if last else len(offsets)
    hid_refs, rest = refs[:n_hid], refs[n_hid + n_alias :]
    if last:
        small_ref, zero_out, one_out, two_out, three_out = rest[:5]
        zero_buf, one_buf, two_buf, three_buf, hid_buf, sems = rest[5:]
    else:
        zero_out, one_out, small_out, zero_buf, one_buf, small_buf, sems = rest
    z, yh, x = position()
    order = [((j % X - x) & (X - 1)) * 2 + (yh ^ (j // X)) for j in range(PLANE)]
    row, col = iotas(512, 128)
    pool1 = one_hot(col == (row >> 7) * 32 + ((row & 63) >> 1), 0.25)
    bias = jnp.concatenate(
        [jnp.transpose(jnp.broadcast_to(bias_ref[n : n + 1, :], (128, 128))) for n in range(2)], axis=0
    )
    bias = jnp.concatenate([bias] * 4, axis=1)
    copies = []

    def send(source, target):
        copies.append(pltpu.make_async_copy(source, target, sems.at[len(copies)]))
        copies[-1].start()

    for n, offset in enumerate(offsets):
        place = (z + (offset + Z)) & (Z - 1)
        if last:
            hid_buf[0:4] = hid_refs[0][...]
            hid_buf[4:8] = hid_refs[1][...]
            hid_ref = hid_buf
        else:
            hid_ref = hid_refs[n]
        ones = []
        for half in range(2):
            hid = jnp.concatenate([hid_ref[order[4 * half + j]] for j in range(4)], axis=1)
            feats = (dot(weight_ref[...], hid) + bias).astype(BF)
            zero = dot(first_ref[...], feats).astype(BF)
            slot = 2 * n + half
            zero_buf[slot] = zero
            send(zero_buf.at[slot], zero_out.at[:, pl.ds(pl.multiple_of(place * 1024 + half * 512, 512), 512)])
            ones.append(dot(zero, pool1).astype(BF))
        one = jnp.concatenate(ones, axis=1)
        one_buf[n] = one
        send(one_buf.at[n], one_out.at[:, pl.ds(pl.multiple_of(place * 256, 256), 256)])
        side = place & 1
        row, col = iotas(256, 128)
        two = dot(one, one_hot(col == side * 64 + (row >> 6) * 16 + ((row & 31) >> 1), 0.25)).astype(BF)
        row, col = iotas(128, 128)
        cell = ((row & 63) >> 5) * 8 + ((row & 15) >> 1)
        three = dot(two, one_hot(((row >> 6) == side) & (col == place * 16 + cell), 0.25)).astype(BF)
        if not last:
            small_buf[n, :, :128] = two
            small_buf[n, :, 128:] = three
            send(small_buf.at[n], small_out.at[place])
    if last:
        for m in range(Z // 2):
            parts = [jnp.where(place == k, two, small_ref[k, :, :128]) for k in (2 * m, 2 * m + 1)]
            two_buf[:, m * 128 : (m + 1) * 128] = parts[0] + parts[1]
        send(two_buf, two_out)
        total = three
        for k in range(Z):
            total = total + jnp.where(place == k, jnp.zeros_like(three), small_ref[k, :, 128:])
        three_buf[...] = total
        send(three_buf, three_out)
    for copy in copies:
        copy.wait()


def planes_call(offsets, hidden, first, proj_weight, proj_bias, outs, last=False):
    count = len(offsets)
    args = [first, proj_weight, proj_bias, *hidden]
    in_specs = [VMEM] * len(args)
    aliases = {}
    if outs is not None:
        shared = 2 if last else 3
        aliases = {len(args) + n: n for n in range(shared)}
        args += list(outs)
        in_specs += [ANYWHERE] * shared + [VMEM] * (len(outs) - shared)
    small = [(512, 512), (512, 128)] if last else [(Z, 512, 256)]
    shapes = [(512, 8192), (512, 2048)] + small
    scratch = [(2 * count, 512, 512), (count, 512, 256)]
    scratch += small + [(8, 128, 128)] if last else [(count, 512, 256)]
    return pl.pallas_call(
        functools.partial(planes_kernel, offsets, last, len(aliases)),
        in_specs=in_specs,
        out_specs=[ANYWHERE] * len(shapes),
        out_shape=[jax.ShapeDtypeStruct(shape, BF) for shape in shapes],
        scratch_shapes=[pltpu.VMEM(shape, BF) for shape in scratch] + [pltpu.SemaphoreType.DMA((5 * count,))],
        input_output_aliases=aliases,
        compiler_params=pltpu.CompilerParams(vmem_limit_bytes=24 << 20),
        cost_estimate=pl.CostEstimate(
            flops=1_400_000_000 * count, bytes_accessed=1_500_000 * count, transcendentals=0
        ),
        name="planes",
    )(*args)


def per_device(images, conv_weight, conv_bias, proj_weight, proj_bias):
    right = [(c, c + 1) for c in range(COLS - 1)]
    down = [(r, r + 1) for r in range(ROWS - 1)]
    diagonal = [(r * COLS + c, (r + 1) * COLS + c + 1) for r in range(ROWS - 1) for c in range(COLS - 1)]
    main, top, left = split_tile(images)
    params = (conv_weight.T, conv_bias[None, :])
    main, top, left, params = lax.optimization_barrier((main, top, left, params))
    corner = lax.ppermute(top, ("rows", "cols"), diagonal)
    top = lax.ppermute(top, "rows", down)
    left = lax.ppermute(left, "cols", right)
    conv_weight, conv_bias = stage(*params)
    hidden_one, hidden_two = hidden_of(main, top, left, corner, conv_weight, conv_bias)

    def along(axis, steps):
        size, stride = {"z": (Z, PLANE), "yh": (YH, X), "x": (X, 1)}[axis]
        target = lambda r: r + ((r // stride + steps) % size - (r // stride) % size) * stride
        return [(r, target(r)) for r in range(ROWS)]

    params = (proj_weight, proj_bias.reshape(2, 128))
    hidden_one, hidden_two, params = lax.optimization_barrier((hidden_one, hidden_two, params))
    other = lax.ppermute(hidden_two, "rows", along("yh", 1))
    proj_weight, proj_bias = stage(*params)
    swapped = lax.ppermute(hidden_one, "cols", [(k, k ^ 1) for k in range(COLS)])
    far = lax.ppermute(jnp.stack([hidden_one, swapped]), "cols", [(k, k ^ 2) for k in range(COLS)])
    other, far, proj_weight, proj_bias = lax.optimization_barrier((other, far, proj_weight, proj_bias))
    pair = jnp.stack([hidden_two, other])
    mine = jnp.concatenate([pair] + [lax.ppermute(pair, "rows", along("x", -s)) for s in range(1, X)])
    first = feats_one((hidden_one, swapped, far), proj_weight, proj_bias)

    call = functools.partial(planes_call, first=first, proj_weight=proj_weight, proj_bias=proj_bias)
    below, above = mine, mine
    outs = call((0,), [mine], outs=None)
    for step in range(1, Z // 2):
        below = lax.ppermute(below, "rows", along("z", 1))
        above = lax.ppermute(above, "rows", along("z", -1))
        outs = call((-step, step), [below, above], outs=outs)
    below = lax.ppermute(below[:4], "rows", along("z", 1))
    above = lax.ppermute(above[4:], "rows", along("z", -1))
    return tuple(call((Z // 2,), [below, above], outs=outs, last=True))


def solution(mesh):
    in_specs = (P(None, None, "rows", "cols"), P(), P(), P(), P())
    out_specs = (P("rows", "cols"), P("rows", "cols"), P("rows", "cols"), P("rows", "cols"))
    return jax.shard_map(
        per_device, mesh=mesh, in_specs=in_specs, out_specs=out_specs, check_vma=False
    )
```
